256 devices in a mesh: keys: 64 (over z, y, core), tiles: 4 (over x).
Axes of the slice: x: 4, y: 4, z: 8, core: 2. Of those that a mesh axis runs over, the one named last changes fastest.
Arguments:
- fact_store: int32 [1048576], P(('keys', 'tiles')), may hold values from 0 to 16383, as said below
- fact_item: int32 [1048576], P(('keys', 'tiles')), may hold values from 0 to 4095, as said below
- store_count: int32 [16384], P('keys'), may hold values from 1 to 64, as said below
- store_table: bfloat16 [16384, 1024], P('keys'), may hold values from -6 to 6
- item_table: bfloat16 [4096, 1024], P('tiles'), may hold values from -6 to 6
Outputs:
- gram_left: float32 [1024, 2048], P('keys', 'tiles')
- gram_items: float32 [1024, 1024], P('keys', 'tiles')
The draws below stay inside these ranges and needn't reach their ends.
Inputs may be any that keep to these rules, and one draw needn't show every extreme that they name: `fact_store`: every fact row held by keys index g names a store of g * 256 to (g + 1) * 256 - 1. `fact_item`: every fact row held by tiles index t names an item of t * 1024 to (t + 1) * 1024 - 1. `store_count`: each a power of two.
All inputs are finite; a program needn't handle non-finite values.
Results may differ from the reference program's by a relative error of at most 0.0003.
Values sent between devices are 32-bit elements; how exact they have to be, the bound alone decides.
A program may use at most 64 MiB of HBM per device.

```python
import jax
import jax.numpy as jnp
from jax import lax

DA = 1024
DB = 1024
KEY_DEV = 256
ITEM_DEV = 1024
ROW_DEV = 4096
KEYS = 16384
ITEMS = 4096
FACT = 1048576


def joint_rows(key):
    base = jax.random.fold_in(key, 7)
    first, second, third, fourth = jax.random.split(base, 4)
    tiles_count = ITEMS // ITEM_DEV
    row = jnp.arange(FACT, dtype=jnp.int32)
    device = row // ROW_DEV
    group = device // tiles_count
    tile = device % tiles_count
    local = jnp.minimum(jax.random.randint(first, (FACT,), 0, KEY_DEV), jax.random.randint(second, (FACT,), 0, KEY_DEV))
    store = group * KEY_DEV + local
    anchor = jax.random.randint(third, (KEYS,), 0, ITEM_DEV)
    offset = jax.random.randint(fourth, (FACT,), 0, 8)
    item = tile * ITEM_DEV + (jnp.take(anchor, store, axis=0) + offset) % ITEM_DEV
    return (store.astype(jnp.int32), item.astype(jnp.int32))


def draw_fact_store(key, part):
    return joint_rows(key)[0]


def draw_fact_item(key, part):
    return joint_rows(key)[1]


def draw_store_count(key, part):
    power = jax.random.randint(jax.random.fold_in(key, 11), (KEYS,), 0, 7)
    counts = jnp.left_shift(jnp.ones((KEYS,), jnp.int32), power)
    return counts.at[0].set(64).at[1].set(1)


def level_of(rng, dims, cuts, low, top_value):
    loudness, own = 1.0, jax.random.fold_in(rng, 6)
    for axis_at, shards_of in cuts:
        draws = jnp.exp(jax.random.uniform(jax.random.fold_in(own, axis_at), (shards_of,), jnp.float32, low / len(cuts), top_value / len(cuts)))
        loudness = loudness * jnp.repeat(draws, dims[axis_at] // shards_of).reshape([-1 if axis == axis_at else 1 for axis in range(len(dims))])
    return loudness


def noise(key, dims, scale, limit, cuts=(), held_as=jnp.bfloat16):
    result = jax.random.normal(key, dims, jnp.float32) * scale
    if len(cuts) > 0:
        result = level_of(key, dims, cuts, -0.22, 0.18) * result
    return jnp.clip(result, min=-limit, max=limit).astype(held_as)


def setup_inputs(seed: int = 0) -> dict:
    seeds = jax.random.split(jax.random.key(seed), 6)
    fact_store = draw_fact_store(jax.random.fold_in(seeds[5], 71), 0)
    fact_item = draw_fact_item(jax.random.fold_in(seeds[5], 71), 0)
    store_count = draw_store_count(jax.random.fold_in(seeds[5], 71), 0)
    store_table = noise(seeds[3], (KEYS, DA), 1.0, 6.0, ((0, 64),))
    item_table = noise(seeds[4], (ITEMS, DB), 1.0, 6.0, ((0, 4),))
    return dict(fact_store=fact_store, fact_item=fact_item, store_count=store_count, store_table=store_table, item_table=item_table)


def reference(fact_store, fact_item, store_count, store_table, item_table):
    row_weight = jnp.take(store_count, fact_store, axis=0).astype(jnp.float32)
    store_weight = jax.ops.segment_sum(row_weight, fact_store, num_segments=KEYS)
    item_weight = jax.ops.segment_sum(row_weight, fact_item, num_segments=ITEMS)
    total = jnp.sum(store_weight)
    flat_index = fact_store * ITEMS + fact_item
    pairs = jax.ops.segment_sum(row_weight, flat_index, num_segments=KEYS * ITEMS).reshape(KEYS, ITEMS)
    item_float = item_table.astype(jnp.float32)
    store_float = store_table.astype(jnp.float32)
    aggregate = jnp.dot(pairs, item_float, precision=lax.Precision.HIGHEST)
    combined = jnp.concatenate([store_weight[:, None] * store_float, aggregate], axis=1)
    gram_left = jnp.dot(store_float.T, combined, precision=lax.Precision.HIGHEST) / total
    gram_items = jnp.dot(item_float.T, item_weight[:, None] * item_float, precision=lax.Precision.HIGHEST) / total
    return gram_left, gram_items
```

```python
import functools

import jax
import jax.numpy as jnp
from jax import lax
from jax.experimental import pallas as pl
from jax.experimental.pallas import tpu as pltpu
from jax.sharding import PartitionSpec as P

MESH = pl.DeviceIdType.MESH
F32 = jnp.float32
BF16 = jnp.bfloat16
CORES = 2
LANES = 128


def nt_dot(a, b):
    return lax.dot_general(a, b, (((1,), (1,)), ((), ())), preferred_element_type=F32)


def dot(a, b):
    return jnp.dot(a, b, preferred_element_type=F32)


def split(x, axis):
    high = x.astype(BF16)
    low = (x - high.astype(F32)).astype(BF16)
    return jnp.concatenate([high, low], axis=axis)


def kernel(
    dims,
    fs_ref, fi_ref, sc_ref, s_hbm, i_hbm,
    left_ref, gram_ref,
    s_ref, i_ref, in_sem,
    counts, pairs, st_ref, scaled,
    n_part, n_recv, n_send_sem, n_recv_sem,
    a_part, a_recv, a_send_sem, a_recv_sem,
    q_part, q_recv, q_send_sem, q_recv_sem,
    y_part, y_recv, y_send_sem, y_recv_sem,
    z_part, z_recv, z_send_sem, z_recv_sem,
    w_part, w_recv, w_send_sem, w_recv_sem,
    g_part, g_recv, g_send_sem, g_recv_sem,
):
    X, Y, Z, key_dev, item_dev, cb, rows = dims
    g = lax.axis_index("keys")
    t = lax.axis_index("tiles")
    c = g % CORES
    y = (g // CORES) % Y
    z = g // (CORES * Y)

    def key(z_at, y_at, c_at):
        return (z_at * Y + y_at) * CORES + c_at

    barrier = pltpu.get_barrier_semaphore()
    greeted = 0
    for dx in range(X):
        for dz in range(Z):
            if dx or dz:
                pl.semaphore_signal(
                    barrier, inc=1, device_id=(key((z + dz) % Z, y, c), (t + dx) % X), device_id_type=MESH
                )
                greeted += 1
    for dy in range(1, Y):
        pl.semaphore_signal(barrier, inc=1, device_id=(key(z, (y + dy) % Y, c), t), device_id_type=MESH)
        greeted += 1
    pl.semaphore_signal(barrier, inc=1, device_id=(key(z, y, 1 - c), t), device_id_type=MESH)
    greeted += 1

    load_i = pltpu.make_async_copy(i_hbm, i_ref, in_sem.at[0])
    load_s = pltpu.make_async_copy(s_hbm, s_ref, in_sem.at[1])
    load_i.start()
    load_s.start()

    half = item_dev // 2
    local_store = fs_ref[...] - g * key_dev
    local_item = fi_ref[...] - t * item_dev
    upper = jnp.where(local_item >= half, 1, 0)
    u = (upper * key_dev + local_store - 256).astype(F32)
    v = (local_item - upper * half - 256).astype(F32)
    iota = (lax.broadcasted_iota(jnp.int32, (512, LANES), 0) - 256).astype(F32).astype(BF16)
    iota = iota.reshape(32, 16, LANES)

    def hot(row):
        row = jnp.broadcast_to(row, (16, LANES)).astype(BF16)
        return jnp.where(iota == row[None], jnp.ones((), BF16), jnp.zeros((), BF16)).reshape(512, LANES)

    per = 8
    for step in range(fs_ref.shape[0] // per):
        at = range(step * per, step * per + per)
        hot_u = jnp.concatenate([hot(u[r : r + 1]) for r in at], axis=1)
        hot_v = jnp.concatenate([hot(v[r : r + 1]) for r in at], axis=1)
        part = nt_dot(hot_u, hot_v)
        if step == 0:
            counts[...] = part
        else:
            counts[...] += part
    pairs[:, :half] = split(counts[:key_dev], 0)
    pairs[:, half:] = split(counts[key_dev:], 0)

    pl.semaphore_wait(barrier, greeted)

    def x_copy(src, dst, send, recv, k):
        return pltpu.make_async_remote_copy(
            src_ref=src, dst_ref=dst, send_sem=send, recv_sem=recv,
            device_id=(g, (t + k) % X), device_id_type=MESH,
        )

    ones = jnp.ones((8, item_dev), BF16)
    row = nt_dot(ones, pairs[...])
    n_part[...] = row[:, :key_dev] + row[:, key_dev:]
    n_copies = []
    for k in range(1, X):
        n_copies.append(x_copy(n_part, n_recv.at[k - 1], n_send_sem.at[k - 1], n_recv_sem.at[k - 1], k))
        n_copies[-1].start()

    load_i.wait()
    a_copies = []
    order = sorted(range(1, X), key=lambda k: -min(k, X - k)) + [0]
    for k in order:
        cols = pl.ds(pl.multiple_of(((t + k) % X) * cb, cb), cb)
        both = dot(pairs[...], i_ref[:, cols])
        a_part[k] = both[:key_dev] + both[key_dev:]
        if k:
            a_copies.append(x_copy(a_part.at[k], a_recv.at[k - 1], a_send_sem.at[k - 1], a_recv_sem.at[k - 1], k))
            a_copies[-1].start()

    count_row = jnp.concatenate([sc_ref[r : r + 1, :] for r in range(key_dev // LANES)], axis=1).astype(F32)
    count_wide = jnp.broadcast_to(count_row, (16, key_dev)).astype(BF16)
    item_row = dot(jnp.concatenate([count_wide, count_wide], axis=1), pairs[...])
    for r in range(item_dev // LANES):
        w_part[0, r : r + 1, :] = item_row[0:1, r * LANES : (r + 1) * LANES]

    def core_copy(src, dst, send, recv):
        return pltpu.make_async_remote_copy(
            src_ref=src, dst_ref=dst, send_sem=send, recv_sem=recv,
            device_id=(key(z, y, 1 - c), t), device_id_type=MESH,
        )

    def y_copy(src, dst, send, recv, k):
        return pltpu.make_async_remote_copy(
            src_ref=src, dst_ref=dst, send_sem=send, recv_sem=recv,
            device_id=(key(z, (y + k) % Y, c), t), device_id_type=MESH,
        )

    def z_copy(src, dst, send, recv, k, tile):
        return pltpu.make_async_remote_copy(
            src_ref=src, dst_ref=dst, send_sem=send, recv_sem=recv,
            device_id=(key((z + k) % Z, y, c), tile), device_id_type=MESH,
        )

    w_core = core_copy(w_part.at[0], w_recv.at[0], w_send_sem.at[0], w_recv_sem.at[0])
    w_core.start()

    load_s.wait()
    st = s_ref[...].T
    st_ref[...] = st.reshape(st_ref.shape)
    scaled[...] = (st * count_wide[0:1]).reshape(scaled.shape)

    def core_stage(kind, left, right):
        q_part[kind, 0] = dot(left(1 - c), right).reshape(q_part.shape[2:])
        copy = core_copy(q_part.at[kind, 0], q_recv.at[kind], q_send_sem.at[kind], q_recv_sem.at[kind])
        copy.start()
        q_part[kind, 1] = dot(left(c), right).reshape(q_part.shape[2:])
        return copy

    def y_stage(kind, copy):
        copy.wait()
        copies = []
        for k in list(range(1, Y)) + [0]:
            at = (y + k) % Y
            y_part[kind, k] = q_part[kind, 1, :, at] + q_recv[kind, :, at]
            if k:
                copies.append(
                    y_copy(
                        y_part.at[kind, k], y_recv.at[kind, k - 1],
                        y_send_sem.at[kind, k - 1], y_recv_sem.at[kind, k - 1], k,
                    )
                )
                copies[-1].start()
        return copies

    def z_stage(kind, copies):
        for copy in copies:
            copy.wait()
        tile = kind * (X // 2) + t // 2
        place = t % 2
        total = y_part[kind, 0]
        for k in range(1, Y):
            total += y_recv[kind, k - 1]
        z_part[kind] = total
        sends = []
        for k in range(Z):
            src = z_part.at[kind, (z + k) % Z]
            dst, recv = z_recv.at[place, k], z_recv_sem.at[place, k]
            copy = z_copy(src, dst, z_send_sem.at[kind, k], recv, k, tile)
            if k:
                copy.start()
                sends.append(copy)
            else:
                pl.when(tile != t)(copy.start)
                pl.when(tile == t)(pltpu.make_async_copy(src, dst, recv).start)
                sends.insert(0, copy)
        return tile, sends

    for copy in n_copies:
        copy.wait()
    store_row = n_part[...]
    for k in range(1, X):
        store_row += n_recv[k - 1]
    weight_row = count_row * store_row[0:1]

    def weighted(side):
        part = st_ref[:, :, side].reshape(-1, key_dev).astype(F32) * weight_row
        return split(part, 1)

    own = s_ref[:, pl.ds(pl.multiple_of(t * cb, cb), cb)]
    store_copy = core_stage(0, weighted, jnp.concatenate([own, own], axis=0))

    w_core.wait()
    w_part[1] = w_part[0] + w_recv[0]
    w_copies = []
    for k in range(1, Y):
        w_copies.append(y_copy(w_part.at[1], w_recv.at[k], w_send_sem.at[k], w_recv_sem.at[k], k))
        w_copies[-1].start()
    store_y = y_stage(0, store_copy)
    for copy in w_copies:
        copy.wait()
    total = w_part[1]
    for k in range(1, Y):
        total += w_recv[k]
    w_part[2] = total
    w_copies = []
    for k in range(1, Z):
        at = Y + k - 1
        w_copies.append(z_copy(w_part.at[2], w_recv.at[at], w_send_sem.at[at], w_recv_sem.at[at], k, t))
        w_copies[-1].start()
    store_tile, store_sends = z_stage(0, store_y)

    for copy in w_copies:
        copy.wait()
    total = w_part[2]
    for k in range(1, Z):
        total += w_recv[Y + k - 1]
    weights = jnp.concatenate([total[r : r + 1, :] for r in range(item_dev // LANES)], axis=1)
    wide = max(rows, LANES)
    block = i_ref[:, pl.ds(pl.multiple_of(((g * rows) // wide) * wide, wide), wide)]
    first = (g * rows) % wide
    pick = lax.broadcasted_iota(jnp.int32, (rows, wide), 1) == lax.broadcasted_iota(jnp.int32, (rows, wide), 0) + first
    picked = nt_dot(jnp.where(pick, 1.0, 0.0).astype(BF16), block)
    both = dot(split(picked * weights, 0), i_ref[...])
    item_rows = both[:rows] + both[rows:]
    for at in range(X):
        g_part[at, :rows] = item_rows[:, at * cb : (at + 1) * cb]
        g_part[at, rows:] = jnp.broadcast_to(jnp.sum(total), (8, cb))
    g_copies = []
    for k in range(1, X):
        g_copies.append(
            x_copy(g_part.at[(t + k) % X], g_recv.at[k - 1], g_send_sem.at[k - 1], g_recv_sem.at[k - 1], k)
        )
        g_copies[-1].start()

    for copy in a_copies:
        copy.wait()
    aggregate = a_part[0]
    for k in range(1, X):
        aggregate += a_recv[k - 1]

    def counted(side):
        part = scaled[:, :, side].reshape(-1, key_dev)
        return jnp.concatenate([part, part], axis=1)

    item_copy = core_stage(1, counted, split(aggregate, 0))
    item_y = y_stage(1, item_copy)
    item_tile, item_sends = z_stage(1, item_y)

    for copy in g_copies:
        copy.wait()
    item_rows = g_part[t]
    for k in range(1, X):
        item_rows += g_recv[k - 1]
    total = item_rows[rows : rows + 1]
    gram_ref[...] = item_rows[:rows] / total

    for place in range(2):
        for k in range(Z):
            z_copy(z_recv.at[place, k], z_recv.at[place, k], z_send_sem.at[0, k], z_recv_sem.at[place, k], k, t).wait_recv()
        block = z_recv[place, 0]
        for k in range(1, Z):
            block += z_recv[place, k]
        left_ref[:, place * cb : (place + 1) * cb] = block / total
    for tile, sends in ((store_tile, store_sends), (item_tile, item_sends)):
        pl.when(tile != t)(sends[0].wait_send)
        for copy in sends[1:]:
            copy.wait_send()


def shards(y_size, fact_store, fact_item, store_count, store_table, item_table):
    key_dev, width_a = store_table.shape
    item_dev, width_b = item_table.shape
    X = lax.axis_size("tiles")
    keys_count = lax.axis_size("keys")
    Y = y_size
    Z = keys_count // (CORES * Y)
    rows, cb = width_a // keys_count, width_b // X
    facts = fact_store.shape[0]
    vmem, dma = pltpu.VMEM, pltpu.SemaphoreType.DMA
    scratch = [
        vmem((key_dev, width_a), BF16), vmem((item_dev, width_b), BF16), dma((2,)),
        vmem((2 * key_dev, item_dev // 2), F32), vmem((2 * key_dev, item_dev), BF16),
        vmem((Z, Y, CORES, rows, key_dev), BF16), vmem((Z, Y, CORES, rows, key_dev), BF16),
        vmem((8, key_dev), F32), vmem((X - 1, 8, key_dev), F32), dma((X - 1,)), dma((X - 1,)),
        vmem((X, key_dev, cb), F32), vmem((X - 1, key_dev, cb), F32), dma((X - 1,)), dma((X - 1,)),
        vmem((2, 2, Z, Y, rows, cb), F32), vmem((2, Z, Y, rows, cb), F32), dma((2,)), dma((2,)),
        vmem((2, Y, Z, rows, cb), F32), vmem((2, Y - 1, Z, rows, cb), F32), dma((2, Y - 1)), dma((2, Y - 1)),
        vmem((2, Z, rows, cb), F32), vmem((2, Z, rows, cb), F32), dma((2, Z)), dma((2, Z)),
        vmem((3, 8, item_dev // 8), F32), vmem((Y + Z - 1, 8, item_dev // 8), F32),
        dma((Y + Z - 1,)), dma((Y + Z - 1,)),
        vmem((X, rows + 8, cb), F32), vmem((X - 1, rows + 8, cb), F32), dma((X - 1,)), dma((X - 1,)),
    ]
    whole = pl.BlockSpec(memory_space=pltpu.VMEM)
    anywhere = pl.BlockSpec(memory_space=pl.ANY)
    return pl.pallas_call(
        functools.partial(kernel, (X, Y, Z, key_dev, item_dev, cb, rows)),
        out_shape=[
            jax.ShapeDtypeStruct((rows, 2 * cb), F32),
            jax.ShapeDtypeStruct((rows, cb), F32),
        ],
        in_specs=[whole, whole, whole, anywhere, anywhere],
        out_specs=[whole, whole],
        scratch_shapes=scratch,
        compiler_params=pltpu.CompilerParams(
            collective_id=0, has_side_effects=True, vmem_limit_bytes=48 * 1024 * 1024
        ),
    )(
        fact_store.reshape(facts // LANES, LANES),
        fact_item.reshape(facts // LANES, LANES),
        store_count.reshape(key_dev // LANES, LANES),
        store_table,
        item_table,
    )


def solution(mesh, y_size=4):
    placed = (
        P(("keys", "tiles")),
        P(("keys", "tiles")),
        P("keys"),
        P("keys", None),
        P("tiles", None),
    )
    return jax.shard_map(
        functools.partial(shards, y_size),
        mesh=mesh,
        in_specs=placed,
        out_specs=(P("keys", "tiles"), P("keys", "tiles")),
        check_vma=False,
    )
```

```python
import functools

import jax
import jax.numpy as jnp
from jax import lax
from jax.experimental import pallas as pl
from jax.experimental.pallas import tpu as pltpu
from jax.sharding import PartitionSpec as P

MESH = pl.DeviceIdType.MESH
F32 = jnp.float32
BF16 = jnp.bfloat16
F8 = jnp.float8_e4m3fn
CORES = 2
LANES = 128


def nt_dot(a, b):
    return lax.dot_general(a, b, (((1,), (1,)), ((), ())), preferred_element_type=F32)


def dot(a, b):
    return jnp.dot(a, b, preferred_element_type=F32)


def split(x, axis):
    high = x.astype(BF16)
    low = (x - high.astype(F32)).astype(BF16)
    return jnp.concatenate([high, low], axis=axis)


def kernel(
    dims,
    fs_hbm, fi_hbm, sc_hbm, s_hbm, i_hbm,
    left_ref, gram_ref,
    fs_ref, fi_ref, sc_ref, s_ref, i_ref, in_sem,
    counts, pairs, st_ref, scaled,
    n_part, n_recv, n_send_sem, n_recv_sem,
    a_part, f_recv, a_recv, f_send_sem, f_recv_sem, a_send_sem, a_recv_sem,
    ss_bufs, sa0_bufs, sa1_bufs,
    w_part, w_recv, w_send_sem, w_recv_sem,
    g_part, g_recv, g_send_sem, g_recv_sem,
):
    X, Y, Z, key_dev, item_dev, cb, rows = dims
    g = lax.axis_index("keys")
    t = lax.axis_index("tiles")
    c = g % CORES
    y = (g // CORES) % Y
    z = g // (CORES * Y)

    def key(z_at, y_at, c_at):
        return (z_at * Y + y_at) * CORES + c_at

    loads = [
        pltpu.make_async_copy(src, dst, in_sem.at[n])
        for n, (src, dst) in enumerate(
            ((fs_hbm, fs_ref), (fi_hbm, fi_ref), (sc_hbm, sc_ref), (i_hbm, i_ref), (s_hbm, s_ref))
        )
    ]
    for load in loads:
        load.start()

    barrier = pltpu.get_barrier_semaphore()
    greeted = 0
    for dx in range(X):
        for dz in range(Z):
            if dx or dz:
                pl.semaphore_signal(
                    barrier, inc=1, device_id=(key((z + dz) % Z, y, c), (t + dx) % X), device_id_type=MESH
                )
                greeted += 1
    for dy in range(1, Y):
        pl.semaphore_signal(barrier, inc=1, device_id=(key(z, (y + dy) % Y, c), t), device_id_type=MESH)
        greeted += 1
    pl.semaphore_signal(barrier, inc=1, device_id=(key(z, y, 1 - c), t), device_id_type=MESH)
    greeted += 1

    loads[0].wait()
    loads[1].wait()
    half = item_dev // 2
    local_store = fs_ref[...] - g * key_dev
    local_item = fi_ref[...] - t * item_dev
    upper = jnp.where(local_item >= half, 1, 0)
    u = (upper * key_dev + local_store - 256).astype(F32)
    v = (local_item - upper * half - 256).astype(F32)
    iota = (lax.broadcasted_iota(jnp.int32, (512, LANES), 0) - 256).astype(F32).astype(BF16)
    iota = iota.reshape(32, 16, LANES)

    def hot(row):
        row = jnp.broadcast_to(row, (16, LANES)).astype(BF16)
        one = jnp.where(iota == row[None], jnp.ones((), BF16), jnp.zeros((), BF16))
        return one.reshape(512, LANES).astype(F8)

    per = 8
    for step in range(fs_ref.shape[0] // per):
        at = range(step * per, step * per + per)
        hot_u = jnp.concatenate([hot(u[r : r + 1]) for r in at], axis=1)
        hot_v = jnp.concatenate([hot(v[r : r + 1]) for r in at], axis=1)
        part = nt_dot(hot_u, hot_v)
        if step == 0:
            counts[...] = part
        else:
            counts[...] += part
    pairs[:, :half] = split(counts[:key_dev], 0)
    pairs[:, half:] = split(counts[key_dev:], 0)

    pl.semaphore_wait(barrier, greeted)

    def remote(src, dst, send, recv, at, tile):
        return pltpu.make_async_remote_copy(
            src_ref=src, dst_ref=dst, send_sem=send, recv_sem=recv, device_id=(at, tile), device_id_type=MESH
        )

    def x_copy(src, dst, send, recv, k):
        return remote(src, dst, send, recv, g, (t + k) % X)

    def core_copy(src, dst, send, recv):
        return remote(src, dst, send, recv, key(z, y, 1 - c), t)

    def y_copy(src, dst, send, recv, k):
        return remote(src, dst, send, recv, key(z, (y + k) % Y, c), t)

    def z_copy(src, dst, send, recv, k, tile):
        return remote(src, dst, send, recv, key((z + k) % Z, y, c), tile)

    ones = jnp.ones((8, item_dev), BF16)
    row = nt_dot(ones, pairs[...])
    n_part[...] = row[:, :key_dev] + row[:, key_dev:]
    n_copies = []
    for k in range(1, X):
        n_copies.append(x_copy(n_part, n_recv.at[k - 1], n_send_sem.at[k - 1], n_recv_sem.at[k - 1], k))
        n_copies[-1].start()

    steps = (1, X - 1)
    chunk = cb // 2
    pair = key_dev // 2

    def half_rows(n):
        return pl.ds(n * pair, pair)

    def forward(q, side):
        return x_copy(
            a_part.at[2, q, half_rows(side)], f_recv.at[side, q],
            f_send_sem.at[side, q], f_recv_sem.at[side, q], steps[side],
        )

    def direct(q, side, n):
        return x_copy(
            a_part.at[steps[side], q, half_rows(n)], a_recv.at[side, q, half_rows(n)],
            a_send_sem.at[side, q, n], a_recv_sem.at[side, q, n], steps[side],
        )

    def aggregate_block(k):
        cols = pl.ds(pl.multiple_of(((t + k) % X) * cb, cb), cb)
        both = dot(pairs[...], i_ref[:, cols])
        both = both[:key_dev] + both[key_dev:]
        for q in range(2):
            a_part[k, q] = both[:, q * chunk : (q + 1) * chunk]

    loads[3].wait()
    aggregate_block(2)
    for side in range(2):
        forward(0, side).start()
    for side in range(2):
        aggregate_block(steps[side])
        direct(0, side, 1 - side).start()
    aggregate_block(0)

    def pass_on(q):
        for side in range(2):
            forward(q, side).wait()
            a_part[steps[side], q, half_rows(side)] += f_recv[side, q]
            direct(q, side, side).start()

    loads[2].wait()
    count_row = jnp.concatenate([sc_ref[r : r + 1, :] for r in range(key_dev // LANES)], axis=1).astype(F32)
    count_wide = jnp.broadcast_to(count_row, (16, key_dev)).astype(BF16)
    item_row = dot(jnp.concatenate([count_wide, count_wide], axis=1), pairs[...])
    for r in range(item_dev // LANES):
        w_part[0, r : r + 1, :] = item_row[0:1, r * LANES : (r + 1) * LANES]
    w_core = core_copy(w_part.at[0], w_recv.at[0], w_send_sem.at[0], w_recv_sem.at[0])
    w_core.start()

    loads[4].wait()
    st = s_ref[...].T
    st_ref[...] = st.reshape(st_ref.shape)
    scaled[...] = (st * count_wide[0:1]).reshape(scaled.shape)

    pass_on(0)
    for side in range(2):
        forward(1, side).start()
    for side in range(2):
        direct(1, side, 1 - side).start()

    def core_stage(bufs, left, right):
        part, recv, send_sem, recv_sem = bufs[:4]
        part[0] = dot(left(1 - c), right).reshape(part.shape[1:])
        copy = core_copy(part.at[0], recv, send_sem, recv_sem)
        copy.start()
        part[1] = dot(left(c), right).reshape(part.shape[1:])

    def y_stage(bufs):
        part, recv, send_sem, recv_sem, y_part, y_recv, y_send_sem, y_recv_sem = bufs[:8]
        core_copy(part.at[0], recv, send_sem, recv_sem).wait()
        copies = []
        for k in (2, 1, 3, 0) if Y == 4 else list(range(1, Y)) + [0]:
            at = (y + k) % Y
            y_part[k] = part[1, :, at] + recv[:, at]
            if k:
                copies.append(
                    y_copy(y_part.at[k], y_recv.at[k - 1], y_send_sem.at[k - 1], y_recv_sem.at[k - 1], k)
                )
                copies[-1].start()
        return copies

    def z_stage(bufs, kind, copies):
        y_part, y_recv = bufs[4:6]
        z_part, z_recv, z_send_sem, z_recv_sem = bufs[8:]
        for copy in copies:
            copy.wait()
        tile = kind * (X // 2) + t // 2
        place = t % 2
        total = y_part[0]
        for k in range(1, Y):
            total += y_recv[k - 1]
        z_part[...] = total
        sends = []
        for k in sorted(range(Z), key=lambda k: -min(k, Z - k)):
            src = z_part.at[(z + k) % Z]
            dst, recv = z_recv.at[place, k], z_recv_sem.at[place, k]
            copy = z_copy(src, dst, z_send_sem.at[k], recv, k, tile)
            if k:
                copy.start()
            else:
                pl.when(tile != t)(copy.start)
                pl.when(tile == t)(pltpu.make_async_copy(src, dst, recv).start)
            sends.append(copy)

        def sent():
            for copy in sends[:-1]:
                copy.wait_send()
            pl.when(tile != t)(sends[-1].wait_send)

        return sent

    for copy in n_copies:
        copy.wait()
    store_row = n_part[...]
    for k in range(1, X):
        store_row += n_recv[k - 1]
    weight_row = count_row * store_row[0:1]

    def weighted(side):
        part = st_ref[:, :, side].reshape(-1, key_dev).astype(F32) * weight_row
        return split(part, 1)

    own = s_ref[:, pl.ds(pl.multiple_of(t * cb, cb), cb)]
    core_stage(ss_bufs, weighted, jnp.concatenate([own, own], axis=0))

    w_core.wait()
    w_part[1] = w_part[0] + w_recv[0]
    w_copies = []
    for k in range(1, Y):
        w_copies.append(y_copy(w_part.at[1], w_recv.at[k], w_send_sem.at[k], w_recv_sem.at[k], k))
        w_copies[-1].start()
    ss_y = y_stage(ss_bufs)

    pass_on(1)

    def counted(side):
        part = scaled[:, :, side].reshape(-1, key_dev)
        return jnp.concatenate([part, part], axis=1)

    def item_columns(q, bufs):
        for side in range(2):
            for n in range(2):
                direct(q, side, n).wait()
        core_stage(bufs, counted, split(a_part[0, q] + (a_recv[0, q] + a_recv[1, q]), 0))

    item_columns(0, sa0_bufs)

    for copy in w_copies:
        copy.wait()
    total = w_part[1]
    for k in range(1, Y):
        total += w_recv[k]
    w_part[2] = total
    w_copies = []
    for k in range(1, Z):
        at = Y + k - 1
        w_copies.append(z_copy(w_part.at[2], w_recv.at[at], w_send_sem.at[at], w_recv_sem.at[at], k, t))
        w_copies[-1].start()

    sa0_y = y_stage(sa0_bufs)
    item_columns(1, sa1_bufs)

    for copy in w_copies:
        copy.wait()
    total = w_part[2]
    for k in range(1, Z):
        total += w_recv[Y + k - 1]
    weights = jnp.concatenate([total[r : r + 1, :] for r in range(item_dev // LANES)], axis=1)
    wide = max(rows, LANES)
    block = i_ref[:, pl.ds(pl.multiple_of(((g * rows) // wide) * wide, wide), wide)]
    first = (g * rows) % wide
    pick = lax.broadcasted_iota(jnp.int32, (rows, wide), 1) == lax.broadcasted_iota(jnp.int32, (rows, wide), 0) + first
    picked = nt_dot(jnp.where(pick, 1.0, 0.0).astype(BF16), block)
    both = dot(split(picked * weights, 0), i_ref[...])
    item_rows = both[:rows] + both[rows:]
    for at in range(X):
        g_part[at, :rows] = item_rows[:, at * cb : (at + 1) * cb]
        g_part[at, rows:] = jnp.broadcast_to(jnp.sum(total), (8, cb))
    g_copies = []
    for k in range(1, X):
        g_copies.append(
            x_copy(g_part.at[(t + k) % X], g_recv.at[k - 1], g_send_sem.at[k - 1], g_recv_sem.at[k - 1], k)
        )
        g_copies[-1].start()

    sa1_y = y_stage(sa1_bufs)
    sents = [z_stage(ss_bufs, 0, ss_y)]
    sents.append(z_stage(sa0_bufs, 1, sa0_y))

    for copy in g_copies:
        copy.wait()
    item_rows = g_part[t]
    for k in range(1, X):
        item_rows += g_recv[k - 1]
    total = item_rows[rows : rows + 1, :chunk]
    gram_ref[...] = item_rows[:rows] / item_rows[rows : rows + 1]

    sents.append(z_stage(sa1_bufs, 1, sa1_y))

    def finish(bufs, col, divisor):
        z_recv, _, z_recv_sem = bufs[9:]
        width = z_recv.shape[-1]
        for place in range(2):
            for k in range(Z):
                z_copy(z_recv.at[place, k], z_recv.at[place, k], bufs[10].at[k], z_recv_sem.at[place, k], k, t).wait_recv()
            block = z_recv[place, 0]
            for k in range(1, Z):
                block += z_recv[place, k]
            left_ref[:, place * cb + col : place * cb + col + width] = block / divisor

    @pl.when(t < X // 2)
    def _():
        finish(ss_bufs, 0, item_rows[rows : rows + 1])

    @pl.when(t >= X // 2)
    def _():
        finish(sa0_bufs, 0, total)
        finish(sa1_bufs, chunk, total)

    for sent in sents:
        sent()


def shards(y_size, fact_store, fact_item, store_count, store_table, item_table):
    key_dev, width_a = store_table.shape
    item_dev, width_b = item_table.shape
    X = lax.axis_size("tiles")
    keys_count = lax.axis_size("keys")
    Y = y_size
    Z = keys_count // (CORES * Y)
    rows, cb = width_a // keys_count, width_b // X
    facts = fact_store.shape[0]
    vmem, dma = pltpu.VMEM, pltpu.SemaphoreType.DMA

    def reduction(width):
        return (
            vmem((2, Z, Y, rows, width), F32), vmem((Z, Y, rows, width), F32), dma(()), dma(()),
            vmem((Y, Z, rows, width), F32), vmem((Y - 1, Z, rows, width), F32), dma((Y - 1,)), dma((Y - 1,)),
            vmem((Z, rows, width), F32), vmem((2, Z, rows, width), F32), dma((Z,)), dma((2, Z)),
        )

    scratch = [
        vmem((facts // LANES, LANES), jnp.int32), vmem((facts // LANES, LANES), jnp.int32),
        vmem((key_dev // LANES, LANES), jnp.int32),
        vmem((key_dev, width_a), BF16), vmem((item_dev, width_b), BF16), dma((5,)),
        vmem((2 * key_dev, item_dev // 2), F32), vmem((2 * key_dev, item_dev), BF16),
        vmem((Z, Y, CORES, rows, key_dev), BF16), vmem((Z, Y, CORES, rows, key_dev), BF16),
        vmem((8, key_dev), F32), vmem((X - 1, 8, key_dev), F32), dma((X - 1,)), dma((X - 1,)),
        vmem((X, 2, key_dev, cb // 2), F32), vmem((2, 2, key_dev // 2, cb // 2), F32),
        vmem((2, 2, key_dev, cb // 2), F32), dma((2, 2)), dma((2, 2)), dma((2, 2, 2)), dma((2, 2, 2)),
        reduction(cb), reduction(cb // 2), reduction(cb // 2),
        vmem((3, 8, item_dev // 8), F32), vmem((Y + Z - 1, 8, item_dev // 8), F32),
        dma((Y + Z - 1,)), dma((Y + Z - 1,)),
        vmem((X, rows + 8, cb), F32), vmem((X - 1, rows + 8, cb), F32), dma((X - 1,)), dma((X - 1,)),
    ]
    whole = pl.BlockSpec(memory_space=pltpu.VMEM)
    hbm = pl.BlockSpec(memory_space=pltpu.HBM)
    return pl.pallas_call(
        functools.partial(kernel, (X, Y, Z, key_dev, item_dev, cb, rows)),
        out_shape=[
            jax.ShapeDtypeStruct((rows, 2 * cb), F32),
            jax.ShapeDtypeStruct((rows, cb), F32),
        ],
        in_specs=[hbm] * 5,
        out_specs=[whole, whole],
        scratch_shapes=scratch,
        compiler_params=pltpu.CompilerParams(
            collective_id=0, has_side_effects=True, vmem_limit_bytes=62 * 1024 * 1024
        ),
    )(
        fact_store.reshape(facts // LANES, LANES),
        fact_item.reshape(facts // LANES, LANES),
        store_count.reshape(key_dev // LANES, LANES),
        store_table,
        item_table,
    )


def solution(mesh, y_size=4):
    placed = (
        P(("keys", "tiles")),
        P(("keys", "tiles")),
        P("keys"),
        P("keys", None),
        P("tiles", None),
    )
    return jax.shard_map(
        functools.partial(shards, y_size),
        mesh=mesh,
        in_specs=placed,
        out_specs=(P("keys", "tiles"), P("keys", "tiles")),
        check_vma=False,
    )
```

```python
import functools

import jax
import jax.numpy as jnp
from jax import lax
from jax.experimental import pallas as pl
from jax.experimental.pallas import tpu as pltpu
from jax.sharding import PartitionSpec as P

MESH = pl.DeviceIdType.MESH
F32 = jnp.float32
BF16 = jnp.bfloat16
F8 = jnp.float8_e4m3fn
CORES = 2
LANES = 128


def nt_dot(a, b):
    return lax.dot_general(a, b, (((1,), (1,)), ((), ())), preferred_element_type=F32)


def dot(a, b):
    return jnp.dot(a, b, preferred_element_type=F32)


def split(x, axis):
    high = x.astype(BF16)
    low = (x - high.astype(F32)).astype(BF16)
    return jnp.concatenate([high, low], axis=axis)


def kernel(
    dims,
    fs_hbm, fi_hbm, sc_hbm, s_hbm, i_hbm,
    left_ref, gram_ref,
    fs_ref, fi_ref, sc_ref, s_ref, i_ref, in_sem,
    counts, pairs, st_ref, scaled,
    n_part, n_recv, n_send_sem, n_recv_sem,
    a_part, f_recv, a_recv, f_send_sem, f_recv_sem, a_send_sem, a_recv_sem,
    ss_bufs, sa0_bufs, sa1_bufs,
    w_part, w_recv, w_send_sem, w_recv_sem,
    g_part, g_recv, g_send_sem, g_recv_sem,
):
    X, Y, Z, key_dev, item_dev, cb, rows = dims
    g = lax.axis_index("keys")
    t = lax.axis_index("tiles")
    c = g % CORES
    y = (g // CORES) % Y
    z = g // (CORES * Y)

    def key(z_at, y_at, c_at):
        return (z_at * Y + y_at) * CORES + c_at

    loads = [
        pltpu.make_async_copy(src, dst, in_sem.at[n])
        for n, (src, dst) in enumerate(
            ((fs_hbm, fs_ref), (fi_hbm, fi_ref), (sc_hbm, sc_ref), (i_hbm, i_ref), (s_hbm, s_ref))
        )
    ]
    for load in loads:
        load.start()

    barrier = pltpu.get_barrier_semaphore()
    greeted = 0
    for dx in range(X):
        for dz in range(Z):
            if dx or dz:
                pl.semaphore_signal(
                    barrier, inc=1, device_id=(key((z + dz) % Z, y, c), (t + dx) % X), device_id_type=MESH
                )
                greeted += 1
    for dy in range(1, Y):
        pl.semaphore_signal(barrier, inc=1, device_id=(key(z, (y + dy) % Y, c), t), device_id_type=MESH)
        greeted += 1
    pl.semaphore_signal(barrier, inc=1, device_id=(key(z, y, 1 - c), t), device_id_type=MESH)
    greeted += 1

    loads[0].wait()
    loads[1].wait()
    half = item_dev // 2
    local_store = fs_ref[...] - g * key_dev
    local_item = fi_ref[...] - t * item_dev
    upper = jnp.where(local_item >= half, 1, 0)
    u = (upper * key_dev + local_store - 256).astype(F32)
    v = (local_item - upper * half - 256).astype(F32)
    iota = (lax.broadcasted_iota(jnp.int32, (512, LANES), 0) - 256).astype(F32).astype(BF16)
    iota = iota.reshape(32, 16, LANES)

    def hot(row):
        row = jnp.broadcast_to(row, (16, LANES)).astype(BF16)
        one = jnp.where(iota == row[None], jnp.ones((), BF16), jnp.zeros((), BF16))
        return one.reshape(512, LANES).astype(F8)

    per = 8
    for step in range(fs_ref.shape[0] // per):
        at = range(step * per, step * per + per)
        hot_u = jnp.concatenate([hot(u[r : r + 1]) for r in at], axis=1)
        hot_v = jnp.concatenate([hot(v[r : r + 1]) for r in at], axis=1)
        part = nt_dot(hot_u, hot_v)
        if step == 0:
            counts[...] = part
        else:
            counts[...] += part
    pairs[:, :half] = split(counts[:key_dev], 0)
    pairs[:, half:] = split(counts[key_dev:], 0)

    pl.semaphore_wait(barrier, greeted)

    def remote(src, dst, send, recv, at, tile):
        return pltpu.make_async_remote_copy(
            src_ref=src, dst_ref=dst, send_sem=send, recv_sem=recv, device_id=(at, tile), device_id_type=MESH
        )

    def x_copy(src, dst, send, recv, k):
        return remote(src, dst, send, recv, g, (t + k) % X)

    def core_copy(src, dst, send, recv):
        return remote(src, dst, send, recv, key(z, y, 1 - c), t)

    def y_copy(src, dst, send, recv, k):
        return remote(src, dst, send, recv, key(z, (y + k) % Y, c), t)

    def z_copy(src, dst, send, recv, k, tile):
        return remote(src, dst, send, recv, key((z + k) % Z, y, c), tile)

    ones = jnp.ones((8, item_dev), BF16)
    row = nt_dot(ones, pairs[...])
    n_part[...] = row[:, :key_dev] + row[:, key_dev:]
    n_copies = []
    for k in range(1, X):
        n_copies.append(x_copy(n_part, n_recv.at[k - 1], n_send_sem.at[k - 1], n_recv_sem.at[k - 1], k))
        n_copies[-1].start()

    steps = (1, X - 1)
    chunk = cb // 2
    pair = key_dev // 2

    def half_rows(n):
        return pl.ds(n * pair, pair)

    def forward(q, side):
        return x_copy(
            a_part.at[2, q, half_rows(side)], f_recv.at[side, q],
            f_send_sem.at[side, q], f_recv_sem.at[side, q], steps[side],
        )

    def direct(q, side, n):
        return x_copy(
            a_part.at[steps[side], q, half_rows(n)], a_recv.at[side, q, half_rows(n)],
            a_send_sem.at[side, q, n], a_recv_sem.at[side, q, n], steps[side],
        )

    def aggregate_block(k):
        cols = pl.ds(pl.multiple_of(((t + k) % X) * cb, cb), cb)
        both = dot(pairs[...], i_ref[:, cols])
        both = both[:key_dev] + both[key_dev:]
        for q in range(2):
            a_part[k, q] = both[:, q * chunk : (q + 1) * chunk]

    loads[3].wait()
    aggregate_block(2)
    for side in range(2):
        forward(0, side).start()
    for side in range(2):
        aggregate_block(steps[side])
        direct(0, side, 1 - side).start()
    aggregate_block(0)

    def pass_on(q):
        for side in range(2):
            forward(q, side).wait()
            a_part[steps[side], q, half_rows(side)] += f_recv[side, q]
            direct(q, side, side).start()

    loads[2].wait()
    count_row = jnp.concatenate([sc_ref[r : r + 1, :] for r in range(key_dev // LANES)], axis=1).astype(F32)
    count_wide = jnp.broadcast_to(count_row, (16, key_dev)).astype(BF16)
    item_row = dot(jnp.concatenate([count_wide, count_wide], axis=1), pairs[...])
    for r in range(item_dev // LANES):
        w_part[0, r : r + 1, :] = item_row[0:1, r * LANES : (r + 1) * LANES]
    w_core = core_copy(w_part.at[0], w_recv.at[0], w_send_sem.at[0], w_recv_sem.at[0])
    w_core.start()

    loads[4].wait()
    st = s_ref[...].T
    st_ref[...] = st.reshape(st_ref.shape)
    scaled[...] = (st * count_wide[0:1]).reshape(scaled.shape)

    pass_on(0)
    for side in range(2):
        forward(1, side).start()
    for side in range(2):
        direct(1, side, 1 - side).start()

    def core_stage(bufs, left, right):
        part, recv, send_sem, recv_sem = bufs[:4]
        part[0] = dot(left(1 - c), right).reshape(part.shape[1:])
        copy = core_copy(part.at[0], recv, send_sem, recv_sem)
        copy.start()
        part[1] = dot(left(c), right).reshape(part.shape[1:])

    def y_stage(bufs):
        part, recv, send_sem, recv_sem, y_part, y_recv, y_send_sem, y_recv_sem = bufs[:8]
        core_copy(part.at[0], recv, send_sem, recv_sem).wait()
        copies = []
        for k in (2, 1, 3, 0) if Y == 4 else list(range(1, Y)) + [0]:
            at = (y + k) % Y
            y_part[k] = part[1, :, at] + recv[:, at]
            if k:
                copies.append(
                    y_copy(y_part.at[k], y_recv.at[k - 1], y_send_sem.at[k - 1], y_recv_sem.at[k - 1], k)
                )
                copies[-1].start()
        return copies

    def z_stage(bufs, kind, copies):
        y_part, y_recv = bufs[4:6]
        z_part, z_recv, z_send_sem, z_recv_sem = bufs[8:]
        for copy in copies:
            copy.wait()
        tile = kind * (X // 2) + t // 2
        place = t % 2
        total = y_part[0]
        for k in range(1, Y):
            total += y_recv[k - 1]
        z_part[...] = total
        sends = []
        for k in sorted(range(Z), key=lambda k: -min(k, Z - k)):
            src = z_part.at[(z + k) % Z]
            dst, recv = z_recv.at[place, k], z_recv_sem.at[place, k]
            copy = z_copy(src, dst, z_send_sem.at[k], recv, k, tile)
            if k:
                copy.start()
            else:
                pl.when(tile != t)(copy.start)
                pl.when(tile == t)(pltpu.make_async_copy(src, dst, recv).start)
            sends.append(copy)

        def sent():
            for copy in sends[:-1]:
                copy.wait_send()
            pl.when(tile != t)(sends[-1].wait_send)

        return sent

    for copy in n_copies:
        copy.wait()
    store_row = n_part[...]
    for k in range(1, X):
        store_row += n_recv[k - 1]
    weight_row = count_row * store_row[0:1]

    def weighted(side):
        part = st_ref[:, :, side].reshape(-1, key_dev).astype(F32) * weight_row
        return split(part, 1)

    own = s_ref[:, pl.ds(pl.multiple_of(t * cb, cb), cb)]
    core_stage(ss_bufs, weighted, jnp.concatenate([own, own], axis=0))

    w_core.wait()
    w_part[1] = w_part[0] + w_recv[0]
    w_copies = []
    for k in range(1, Y):
        w_copies.append(y_copy(w_part.at[1], w_recv.at[k], w_send_sem.at[k], w_recv_sem.at[k], k))
        w_copies[-1].start()
    ss_y = y_stage(ss_bufs)

    pass_on(1)

    def counted(side):
        part = scaled[:, :, side].reshape(-1, key_dev)
        return jnp.concatenate([part, part], axis=1)

    def item_columns(q, bufs):
        for side in range(2):
            for n in range(2):
                direct(q, side, n).wait()
        core_stage(bufs, counted, split(a_part[0, q] + (a_recv[0, q] + a_recv[1, q]), 0))

    item_columns(0, sa0_bufs)

    for copy in w_copies:
        copy.wait()
    total = w_part[1]
    for k in range(1, Y):
        total += w_recv[k]
    w_part[2] = total
    w_copies = []
    for k in range(1, Z):
        at = Y + k - 1
        w_copies.append(z_copy(w_part.at[2], w_recv.at[at], w_send_sem.at[at], w_recv_sem.at[at], k, t))
        w_copies[-1].start()

    sa0_y = y_stage(sa0_bufs)
    item_columns(1, sa1_bufs)

    for copy in w_copies:
        copy.wait()
    total = w_part[2]
    for k in range(1, Z):
        total += w_recv[Y + k - 1]
    weights = jnp.concatenate([total[r : r + 1, :] for r in range(item_dev // LANES)], axis=1)
    wide = max(rows, LANES)
    block = i_ref[:, pl.ds(pl.multiple_of(((g * rows) // wide) * wide, wide), wide)]
    first = (g * rows) % wide
    pick = lax.broadcasted_iota(jnp.int32, (rows, wide), 1) == lax.broadcasted_iota(jnp.int32, (rows, wide), 0) + first
    picked = nt_dot(jnp.where(pick, 1.0, 0.0).astype(BF16), block)
    both = dot(split(picked * weights, 0), i_ref[...])
    item_rows = both[:rows] + both[rows:]
    for at in range(X):
        g_part[at, :rows] = item_rows[:, at * cb : (at + 1) * cb]
        g_part[at, rows:] = jnp.broadcast_to(jnp.sum(total), (8, cb))
    g_copies = []
    for k in range(1, X):
        g_copies.append(
            x_copy(g_part.at[(t + k) % X], g_recv.at[k - 1], g_send_sem.at[k - 1], g_recv_sem.at[k - 1], k)
        )
        g_copies[-1].start()

    sa1_y = y_stage(sa1_bufs)
    sents = [z_stage(ss_bufs, 0, ss_y)]
    sents.append(z_stage(sa0_bufs, 1, sa0_y))

    for copy in g_copies:
        copy.wait()
    item_rows = g_part[t]
    for k in range(1, X):
        item_rows += g_recv[k - 1]
    total = item_rows[rows : rows + 1, :chunk]
    gram_ref[...] = item_rows[:rows] / item_rows[rows : rows + 1]

    sents.append(z_stage(sa1_bufs, 1, sa1_y))

    def finish(bufs, col, divisor):
        z_recv, _, z_recv_sem = bufs[9:]
        width = z_recv.shape[-1]
        for place in range(2):
            for k in range(Z):
                z_copy(z_recv.at[place, k], z_recv.at[place, k], bufs[10].at[k], z_recv_sem.at[place, k], k, t).wait_recv()
            block = z_recv[place, 0]
            for k in range(1, Z):
                block += z_recv[place, k]
            left_ref[:, place * cb + col : place * cb + col + width] = block / divisor

    @pl.when(t < X // 2)
    def _():
        finish(ss_bufs, 0, item_rows[rows : rows + 1])

    @pl.when(t >= X // 2)
    def _():
        finish(sa0_bufs, 0, total)
        finish(sa1_bufs, chunk, total)

    for sent in sents:
        sent()


def shards(y_size, fact_store, fact_item, store_count, store_table, item_table):
    key_dev, width_a = store_table.shape
    item_dev, width_b = item_table.shape
    X = lax.axis_size("tiles")
    keys_count = lax.axis_size("keys")
    Y = y_size
    Z = keys_count // (CORES * Y)
    rows, cb = width_a // keys_count, width_b // X
    facts = fact_store.shape[0]
    vmem, dma = pltpu.VMEM, pltpu.SemaphoreType.DMA

    def reduction(width):
        return (
            vmem((2, Z, Y, rows, width), F32), vmem((Z, Y, rows, width), F32), dma(()), dma(()),
            vmem((Y, Z, rows, width), F32), vmem((Y - 1, Z, rows, width), F32), dma((Y - 1,)), dma((Y - 1,)),
            vmem((Z, rows, width), F32), vmem((2, Z, rows, width), F32), dma((Z,)), dma((2, Z)),
        )

    scratch = [
        vmem((facts // LANES, LANES), jnp.int32), vmem((facts // LANES, LANES), jnp.int32),
        vmem((key_dev // LANES, LANES), jnp.int32),
        vmem((key_dev, width_a), BF16), vmem((item_dev, width_b), BF16), dma((5,)),
        vmem((2 * key_dev, item_dev // 2), F32), vmem((2 * key_dev, item_dev), BF16),
        vmem((Z, Y, CORES, rows, key_dev), BF16), vmem((Z, Y, CORES, rows, key_dev), BF16),
        vmem((8, key_dev), F32), vmem((X - 1, 8, key_dev), F32), dma((X - 1,)), dma((X - 1,)),
        vmem((X, 2, key_dev, cb // 2), F32), vmem((2, 2, key_dev // 2, cb // 2), F32),
        vmem((2, 2, key_dev, cb // 2), F32), dma((2, 2)), dma((2, 2)), dma((2, 2, 2)), dma((2, 2, 2)),
        reduction(cb), reduction(cb // 2), reduction(cb // 2),
        vmem((3, 8, item_dev // 8), F32), vmem((Y + Z - 1, 8, item_dev // 8), F32),
        dma((Y + Z - 1,)), dma((Y + Z - 1,)),
        vmem((X, rows + 8, cb), F32), vmem((X - 1, rows + 8, cb), F32), dma((X - 1,)), dma((X - 1,)),
    ]
    whole = pl.BlockSpec(memory_space=pltpu.VMEM)
    hbm = pl.BlockSpec(memory_space=pltpu.HBM)
    return pl.pallas_call(
        functools.partial(kernel, (X, Y, Z, key_dev, item_dev, cb, rows)),
        out_shape=[
            jax.ShapeDtypeStruct((rows, 2 * cb), F32),
            jax.ShapeDtypeStruct((rows, cb), F32),
        ],
        in_specs=[hbm] * 5,
        out_specs=[whole, whole],
        scratch_shapes=scratch,
        compiler_params=pltpu.CompilerParams(
            collective_id=0, has_side_effects=True, vmem_limit_bytes=40 * 1024 * 1024
        ),
    )(
        *(
            pltpu.with_memory_space_constraint(operand, pltpu.HBM)
            for operand in (
                fact_store.reshape(facts // LANES, LANES),
                fact_item.reshape(facts // LANES, LANES),
                store_count.reshape(key_dev // LANES, LANES),
                store_table,
                item_table,
            )
        )
    )


def solution(mesh, y_size=4):
    placed = (
        P(("keys", "tiles")),
        P(("keys", "tiles")),
        P("keys"),
        P("keys", None),
        P("tiles", None),
    )
    return jax.shard_map(
        functools.partial(shards, y_size),
        mesh=mesh,
        in_specs=placed,
        out_specs=(P("keys", "tiles"), P("keys", "tiles")),
        check_vma=False,
    )
```

```python
import functools

import jax
import jax.numpy as jnp
from jax import lax
from jax.experimental import pallas as pl
from jax.experimental.pallas import tpu as pltpu
from jax.sharding import PartitionSpec as P

MESH = pl.DeviceIdType.MESH
F32 = jnp.float32
BF16 = jnp.bfloat16
F8 = jnp.float8_e4m3fn
CORES = 2
LANES = 128


def nt_dot(a, b):
    return lax.dot_general(a, b, (((1,), (1,)), ((), ())), preferred_element_type=F32)


def dot(a, b):
    return jnp.dot(a, b, preferred_element_type=F32)


def split(x, axis):
    high = x.astype(BF16)
    low = (x - high.astype(F32)).astype(BF16)
    return jnp.concatenate([high, low], axis=axis)


def kernel(
    dims,
    fs_hbm, fi_hbm, sc_hbm, s_hbm, i_hbm,
    left_ref, gram_ref,
    fs_ref, fi_ref, sc_ref, s_ref, i_ref, in_sem,
    counts, pairs, st_ref, scaled,
    n_part, n_recv, n_send_sem, n_recv_sem,
    a_part, f_recv, a_recv, f_send_sem, f_recv_sem, a_send_sem, a_recv_sem,
    ss_bufs, sa0_bufs, sa1_bufs,
    w_part, w_recv, w_send_sem, w_recv_sem,
    g_part, g_recv, g_send_sem, g_recv_sem,
):
    X, Y, Z, key_dev, item_dev, cb, rows = dims
    g = lax.axis_index("keys")
    t = lax.axis_index("tiles")
    c = g % CORES
    y = (g // CORES) % Y
    z = g // (CORES * Y)

    def store_block(tile):
        upper = tile // 2
        return (1 - upper) * 2 * tile + upper * (7 - 2 * tile)

    def item_block(tile):
        upper = tile // 2
        return (1 - upper) * (3 - 2 * tile) + upper * (2 * tile - 4)

    def key(z_at, y_at, c_at):
        return (z_at * Y + y_at) * CORES + c_at

    loads = [
        pltpu.make_async_copy(src, dst, in_sem.at[n])
        for n, (src, dst) in enumerate(
            ((fs_hbm, fs_ref), (fi_hbm, fi_ref), (sc_hbm, sc_ref), (i_hbm, i_ref), (s_hbm, s_ref))
        )
    ]
    for load in loads:
        load.start()

    barrier = pltpu.get_barrier_semaphore()
    greeted = 0
    for dx in range(X):
        for dz in range(Z):
            if dx or dz:
                pl.semaphore_signal(
                    barrier, inc=1, device_id=(key((z + dz) % Z, y, c), (t + dx) % X), device_id_type=MESH
                )
                greeted += 1
    for dy in range(1, Y):
        pl.semaphore_signal(barrier, inc=1, device_id=(key(z, (y + dy) % Y, c), t), device_id_type=MESH)
        greeted += 1
    pl.semaphore_signal(barrier, inc=1, device_id=(key(z, y, 1 - c), t), device_id_type=MESH)
    greeted += 1

    loads[0].wait()
    loads[1].wait()
    half = item_dev // 2
    local_store = fs_ref[...] - g * key_dev
    local_item = fi_ref[...] - t * item_dev
    upper = jnp.where(local_item >= half, 1, 0)
    u = (upper * key_dev + local_store - 256).astype(F32)
    v = (local_item - upper * half - 256).astype(F32)
    iota = (lax.broadcasted_iota(jnp.int32, (512, LANES), 0) - 256).astype(F32).astype(BF16)
    iota = iota.reshape(32, 16, LANES)

    def hot(row):
        row = jnp.broadcast_to(row, (16, LANES)).astype(BF16)
        one = jnp.where(iota == row[None], jnp.ones((), BF16), jnp.zeros((), BF16))
        return one.reshape(512, LANES).astype(F8)

    per = 8
    for step in range(fs_ref.shape[0] // per):
        at = range(step * per, step * per + per)
        hot_u = jnp.concatenate([hot(u[r : r + 1]) for r in at], axis=1)
        hot_v = jnp.concatenate([hot(v[r : r + 1]) for r in at], axis=1)
        part = nt_dot(hot_u, hot_v)
        if step == 0:
            counts[...] = part
        else:
            counts[...] += part
    pairs[:, :half] = split(counts[:key_dev], 0)
    pairs[:, half:] = split(counts[key_dev:], 0)

    pl.semaphore_wait(barrier, greeted)

    def remote(src, dst, send, recv, at, tile):
        return pltpu.make_async_remote_copy(
            src_ref=src, dst_ref=dst, send_sem=send, recv_sem=recv, device_id=(at, tile), device_id_type=MESH
        )

    def x_copy(src, dst, send, recv, k):
        return remote(src, dst, send, recv, g, (t + k) % X)

    def core_copy(src, dst, send, recv):
        return remote(src, dst, send, recv, key(z, y, 1 - c), t)

    def y_copy(src, dst, send, recv, k):
        return remote(src, dst, send, recv, key(z, (y + k) % Y, c), t)

    def z_copy(src, dst, send, recv, k, tile):
        return remote(src, dst, send, recv, key((z + k) % Z, y, c), tile)

    ones = jnp.ones((8, item_dev), BF16)
    row = nt_dot(ones, pairs[...])
    n_part[...] = row[:, :key_dev] + row[:, key_dev:]
    n_copies = []
    for k in range(1, X):
        n_copies.append(x_copy(n_part, n_recv.at[k - 1], n_send_sem.at[k - 1], n_recv_sem.at[k - 1], k))
        n_copies[-1].start()

    steps = (1, X - 1)
    chunk = cb // 2
    pair = key_dev // 2

    def half_rows(n):
        return pl.ds(n * pair, pair)

    def forward(q, side):
        return x_copy(
            a_part.at[2, q, half_rows(side)], f_recv.at[side, q],
            f_send_sem.at[side, q], f_recv_sem.at[side, q], steps[side],
        )

    def direct(q, side, n):
        return x_copy(
            a_part.at[steps[side], q, half_rows(n)], a_recv.at[side, q, half_rows(n)],
            a_send_sem.at[side, q, n], a_recv_sem.at[side, q, n], steps[side],
        )

    def aggregate_block(k):
        cols = pl.ds(pl.multiple_of(item_block((t + k) % X) * cb, cb), cb)
        both = dot(pairs[...], i_ref[:, cols])
        both = both[:key_dev] + both[key_dev:]
        for q in range(2):
            a_part[k, q] = both[:, q * chunk : (q + 1) * chunk]

    loads[3].wait()
    aggregate_block(2)
    for side in range(2):
        forward(0, side).start()
    for side in range(2):
        aggregate_block(steps[side])
        direct(0, side, 1 - side).start()
    aggregate_block(0)

    def pass_on(q):
        for side in range(2):
            forward(q, side).wait()
            a_part[steps[side], q, half_rows(side)] += f_recv[side, q]
            direct(q, side, side).start()

    loads[2].wait()
    count_row = jnp.concatenate([sc_ref[r : r + 1, :] for r in range(key_dev // LANES)], axis=1).astype(F32)
    count_wide = jnp.broadcast_to(count_row, (16, key_dev)).astype(BF16)
    item_row = dot(jnp.concatenate([count_wide, count_wide], axis=1), pairs[...])
    for r in range(item_dev // LANES):
        w_part[0, r : r + 1, :] = item_row[0:1, r * LANES : (r + 1) * LANES]
    w_core = core_copy(w_part.at[0], w_recv.at[0], w_send_sem.at[0], w_recv_sem.at[0])
    w_core.start()

    loads[4].wait()
    st = s_ref[...].T
    st_ref[...] = st.reshape(st_ref.shape)
    scaled[...] = (st * count_wide[0:1]).reshape(scaled.shape)

    pass_on(0)
    for side in range(2):
        forward(1, side).start()
    for side in range(2):
        direct(1, side, 1 - side).start()

    def core_stage(bufs, left, right):
        part, recv, send_sem, recv_sem = bufs[:4]
        part[0] = dot(left(1 - c), right).reshape(part.shape[1:])
        copy = core_copy(part.at[0], recv, send_sem, recv_sem)
        copy.start()
        part[1] = dot(left(c), right).reshape(part.shape[1:])

    def y_stage(bufs):
        part, recv, send_sem, recv_sem, y_part, y_recv, y_send_sem, y_recv_sem = bufs[:8]
        core_copy(part.at[0], recv, send_sem, recv_sem).wait()
        copies = []
        for k in (2, 1, 3, 0) if Y == 4 else list(range(1, Y)) + [0]:
            at = (y + k) % Y
            y_part[k] = part[1, :, at] + recv[:, at]
            if k:
                copies.append(
                    y_copy(y_part.at[k], y_recv.at[k - 1], y_send_sem.at[k - 1], y_recv_sem.at[k - 1], k)
                )
                copies[-1].start()
        return copies

    def z_stage(bufs, kind, copies):
        y_part, y_recv = bufs[4:6]
        z_part, z_recv, z_send_sem, z_recv_sem = bufs[8:]
        for copy in copies:
            copy.wait()
        block = item_block(t) if kind else store_block(t)
        tile = kind * (X // 2) + block // 2
        place = block % 2
        total = y_part[0]
        for k in range(1, Y):
            total += y_recv[k - 1]
        z_part[...] = total
        sends = []
        for k in sorted(range(Z), key=lambda k: -min(k, Z - k)):
            src = z_part.at[(z + k) % Z]
            dst, recv = z_recv.at[place, k], z_recv_sem.at[place, k]
            copy = z_copy(src, dst, z_send_sem.at[k], recv, k, tile)
            if k:
                copy.start()
            else:
                pl.when(tile != t)(copy.start)
                pl.when(tile == t)(pltpu.make_async_copy(src, dst, recv).start)
            sends.append(copy)

        def sent():
            for copy in sends[:-1]:
                copy.wait_send()
            pl.when(tile != t)(sends[-1].wait_send)

        return sent

    for copy in n_copies:
        copy.wait()
    store_row = n_part[...]
    for k in range(1, X):
        store_row += n_recv[k - 1]
    weight_row = count_row * store_row[0:1]

    def weighted(side):
        part = st_ref[:, :, side].reshape(-1, key_dev).astype(F32) * weight_row
        return split(part, 1)

    own = s_ref[:, pl.ds(pl.multiple_of(store_block(t) * cb, cb), cb)]
    core_stage(ss_bufs, weighted, jnp.concatenate([own, own], axis=0))

    w_core.wait()
    w_part[1] = w_part[0] + w_recv[0]
    w_copies = []
    for k in range(1, Y):
        w_copies.append(y_copy(w_part.at[1], w_recv.at[k], w_send_sem.at[k], w_recv_sem.at[k], k))
        w_copies[-1].start()
    ss_y = y_stage(ss_bufs)

    pass_on(1)

    def counted(side):
        part = scaled[:, :, side].reshape(-1, key_dev)
        return jnp.concatenate([part, part], axis=1)

    def item_columns(q, bufs):
        for side in range(2):
            for n in range(2):
                direct(q, side, n).wait()
        core_stage(bufs, counted, split(a_part[0, q] + (a_recv[0, q] + a_recv[1, q]), 0))

    item_columns(0, sa0_bufs)

    for copy in w_copies:
        copy.wait()
    total = w_part[1]
    for k in range(1, Y):
        total += w_recv[k]
    w_part[2] = total
    w_copies = []
    for k in range(1, Z):
        at = Y + k - 1
        w_copies.append(z_copy(w_part.at[2], w_recv.at[at], w_send_sem.at[at], w_recv_sem.at[at], k, t))
        w_copies[-1].start()

    sa0_y = y_stage(sa0_bufs)
    item_columns(1, sa1_bufs)

    for copy in w_copies:
        copy.wait()
    total = w_part[2]
    for k in range(1, Z):
        total += w_recv[Y + k - 1]
    weights = jnp.concatenate([total[r : r + 1, :] for r in range(item_dev // LANES)], axis=1)
    wide = max(rows, LANES)
    block = i_ref[:, pl.ds(pl.multiple_of(((g * rows) // wide) * wide, wide), wide)]
    first = (g * rows) % wide
    pick = lax.broadcasted_iota(jnp.int32, (rows, wide), 1) == lax.broadcasted_iota(jnp.int32, (rows, wide), 0) + first
    picked = nt_dot(jnp.where(pick, 1.0, 0.0).astype(BF16), block)
    both = dot(split(picked * weights, 0), i_ref[...])
    item_rows = both[:rows] + both[rows:]
    for at in range(X):
        g_part[at, :rows] = item_rows[:, at * cb : (at + 1) * cb]
        g_part[at, rows:] = jnp.broadcast_to(jnp.sum(total), (8, cb))
    g_copies = []
    for k in range(1, X):
        g_copies.append(
            x_copy(g_part.at[(t + k) % X], g_recv.at[k - 1], g_send_sem.at[k - 1], g_recv_sem.at[k - 1], k)
        )
        g_copies[-1].start()

    sa1_y = y_stage(sa1_bufs)
    sents = [z_stage(ss_bufs, 0, ss_y)]
    sents.append(z_stage(sa0_bufs, 1, sa0_y))

    for copy in g_copies:
        copy.wait()
    item_rows = g_part[t]
    for k in range(1, X):
        item_rows += g_recv[k - 1]
    total = item_rows[rows : rows + 1, :chunk]
    gram_ref[...] = item_rows[:rows] / item_rows[rows : rows + 1]

    sents.append(z_stage(sa1_bufs, 1, sa1_y))

    def finish(bufs, col, divisor):
        z_recv, _, z_recv_sem = bufs[9:]
        width = z_recv.shape[-1]
        for place in range(2):
            for k in range(Z):
                z_copy(z_recv.at[place, k], z_recv.at[place, k], bufs[10].at[k], z_recv_sem.at[place, k], k, t).wait_recv()
            block = z_recv[place, 0]
            for k in range(1, Z):
                block += z_recv[place, k]
            left_ref[:, place * cb + col : place * cb + col + width] = block / divisor

    @pl.when(t < X // 2)
    def _():
        finish(ss_bufs, 0, item_rows[rows : rows + 1])

    @pl.when(t >= X // 2)
    def _():
        finish(sa0_bufs, 0, total)
        finish(sa1_bufs, chunk, total)

    for sent in sents:
        sent()


def shards(y_size, fact_store, fact_item, store_count, store_table, item_table):
    key_dev, width_a = store_table.shape
    item_dev, width_b = item_table.shape
    X = lax.axis_size("tiles")
    keys_count = lax.axis_size("keys")
    Y = y_size
    Z = keys_count // (CORES * Y)
    rows, cb = width_a // keys_count, width_b // X
    facts = fact_store.shape[0]
    vmem, dma = pltpu.VMEM, pltpu.SemaphoreType.DMA

    def reduction(width):
        return (
            vmem((2, Z, Y, rows, width), F32), vmem((Z, Y, rows, width), F32), dma(()), dma(()),
            vmem((Y, Z, rows, width), F32), vmem((Y - 1, Z, rows, width), F32), dma((Y - 1,)), dma((Y - 1,)),
            vmem((Z, rows, width), F32), vmem((2, Z, rows, width), F32), dma((Z,)), dma((2, Z)),
        )

    scratch = [
        vmem((facts // LANES, LANES), jnp.int32), vmem((facts // LANES, LANES), jnp.int32),
        vmem((key_dev // LANES, LANES), jnp.int32),
        vmem((key_dev, width_a), BF16), vmem((item_dev, width_b), BF16), dma((5,)),
        vmem((2 * key_dev, item_dev // 2), F32), vmem((2 * key_dev, item_dev), BF16),
        vmem((Z, Y, CORES, rows, key_dev), BF16), vmem((Z, Y, CORES, rows, key_dev), BF16),
        vmem((8, key_dev), F32), vmem((X - 1, 8, key_dev), F32), dma((X - 1,)), dma((X - 1,)),
        vmem((X, 2, key_dev, cb // 2), F32), vmem((2, 2, key_dev // 2, cb // 2), F32),
        vmem((2, 2, key_dev, cb // 2), F32), dma((2, 2)), dma((2, 2)), dma((2, 2, 2)), dma((2, 2, 2)),
        reduction(cb), reduction(cb // 2), reduction(cb // 2),
        vmem((3, 8, item_dev // 8), F32), vmem((Y + Z - 1, 8, item_dev // 8), F32),
        dma((Y + Z - 1,)), dma((Y + Z - 1,)),
        vmem((X, rows + 8, cb), F32), vmem((X - 1, rows + 8, cb), F32), dma((X - 1,)), dma((X - 1,)),
    ]
    whole = pl.BlockSpec(memory_space=pltpu.VMEM)
    hbm = pl.BlockSpec(memory_space=pltpu.HBM)
    return pl.pallas_call(
        functools.partial(kernel, (X, Y, Z, key_dev, item_dev, cb, rows)),
        out_shape=[
            jax.ShapeDtypeStruct((rows, 2 * cb), F32),
            jax.ShapeDtypeStruct((rows, cb), F32),
        ],
        in_specs=[hbm] * 5,
        out_specs=[whole, whole],
        scratch_shapes=scratch,
        compiler_params=pltpu.CompilerParams(
            collective_id=0, has_side_effects=True, vmem_limit_bytes=40 * 1024 * 1024
        ),
    )(
        *(
            pltpu.with_memory_space_constraint(operand, pltpu.HBM)
            for operand in (
                fact_store.reshape(facts // LANES, LANES),
                fact_item.reshape(facts // LANES, LANES),
                store_count.reshape(key_dev // LANES, LANES),
                store_table,
                item_table,
            )
        )
    )


def solution(mesh, y_size=4):
    placed = (
        P(("keys", "tiles")),
        P(("keys", "tiles")),
        P("keys"),
        P("keys", None),
        P("tiles", None),
    )
    return jax.shard_map(
        functools.partial(shards, y_size),
        mesh=mesh,
        in_specs=placed,
        out_specs=(P("keys", "tiles"), P("keys", "tiles")),
        check_vma=False,
    )
```

```python
import functools

import jax
import jax.numpy as jnp
from jax import lax
from jax.experimental import pallas as pl
from jax.experimental.pallas import tpu as pltpu
from jax.sharding import PartitionSpec as P

MESH = pl.DeviceIdType.MESH
F32 = jnp.float32
BF16 = jnp.bfloat16
F8 = jnp.float8_e4m3fn
CORES = 2
LANES = 128


def nt_dot(a, b):
    return lax.dot_general(a, b, (((1,), (1,)), ((), ())), preferred_element_type=F32)


def dot(a, b):
    return jnp.dot(a, b, preferred_element_type=F32)


def split(x, axis):
    high = x.astype(BF16)
    low = (x - high.astype(F32)).astype(BF16)
    return jnp.concatenate([high, low], axis=axis)


def kernel(
    dims,
    fs_hbm, fi_hbm, sc_hbm, s_hbm, i_hbm,
    left_ref, gram_ref,
    fs_ref, fi_ref, sc_ref, s_ref, i_ref, in_sem,
    counts, pairs, st_ref, scaled,
    n_part, n_recv, n_send_sem, n_recv_sem,
    a_part, f_recv, a_recv, f_send_sem, f_recv_sem, a_send_sem, a_recv_sem,
    ss_bufs, sa0_bufs, sa1_bufs,
    w_part, w_recv, w_send_sem, w_recv_sem,
    g_part, g_recv, g_send_sem, g_recv_sem,
):
    X, Y, Z, key_dev, item_dev, cb, rows = dims
    g = lax.axis_index("keys")
    t = lax.axis_index("tiles")
    c = g % CORES
    y = (g // CORES) % Y
    z = g // (CORES * Y)

    def store_block(tile):
        upper = tile // 2
        return (1 - upper) * 2 * tile + upper * (7 - 2 * tile)

    def item_block(tile):
        upper = tile // 2
        return (1 - upper) * (3 - 2 * tile) + upper * (2 * tile - 4)

    def key(z_at, y_at, c_at):
        return (z_at * Y + y_at) * CORES + c_at

    loads = [
        pltpu.make_async_copy(src, dst, in_sem.at[n])
        for n, (src, dst) in enumerate(
            ((fs_hbm, fs_ref), (fi_hbm, fi_ref), (sc_hbm, sc_ref), (i_hbm, i_ref), (s_hbm, s_ref))
        )
    ]
    for load in loads:
        load.start()

    barrier = pltpu.get_barrier_semaphore()
    greeted = 0
    partners = [(key(z, y, c), (t + dx) % X) for dx in range(1, X)] + [(key(z, y, 1 - c), t)]
    partners += [(key(z, (y + dy) % Y, c), t) for dy in range(1, Y)]
    partners += [(key((z + dz) % Z, y, c), (t + dx) % X) for dx in range(X) for dz in range(1, Z)]
    for at, tile in partners:
        pl.semaphore_signal(barrier, inc=1, device_id=(at, tile), device_id_type=MESH)
        greeted += 1

    loads[0].wait()
    loads[1].wait()
    half = item_dev // 2
    local_store = fs_ref[...] - g * key_dev
    local_item = fi_ref[...] - t * item_dev
    upper = jnp.where(local_item >= half, 1, 0)
    u = (upper * key_dev + local_store - 256).astype(F32)
    v = (local_item - upper * half - 256).astype(F32)
    iota = (lax.broadcasted_iota(jnp.int32, (512, LANES), 0) - 256).astype(F32).astype(BF16)
    iota = iota.reshape(32, 16, LANES)

    def hot(row):
        row = jnp.broadcast_to(row, (16, LANES)).astype(BF16)
        one = jnp.where(iota == row[None], jnp.ones((), BF16), jnp.zeros((), BF16))
        return one.reshape(512, LANES).astype(F8)

    store_low = (local_store % LANES).astype(F32)
    store_high = (local_store // LANES).astype(F32)
    count = lax.broadcasted_iota(jnp.int32, (LANES, LANES), 0).astype(F32).astype(BF16).reshape(-1, 16, LANES)

    def hot_store(row, groups):
        row = jnp.broadcast_to(row, (16, LANES)).astype(BF16)
        one = jnp.where(count[:groups] == row[None], jnp.ones((), BF16), jnp.zeros((), BF16))
        return one.reshape(16 * groups, LANES)

    steps = fs_ref.shape[0]
    n_part[...] = nt_dot(
        jnp.concatenate([hot_store(store_high[r : r + 1], 1) for r in range(steps)], axis=1),
        jnp.concatenate([hot_store(store_low[r : r + 1], LANES // 16) for r in range(steps)], axis=1),
    )

    per = 8
    for step in range(steps // per):
        at = range(step * per, step * per + per)
        hot_u = jnp.concatenate([hot(u[r : r + 1]) for r in at], axis=1)
        hot_v = jnp.concatenate([hot(v[r : r + 1]) for r in at], axis=1)
        part = nt_dot(hot_u, hot_v)
        if step == 0:
            counts[...] = part
            loads[2].wait()
            loads[4].wait()
            count_row = jnp.concatenate([sc_ref[r : r + 1, :] for r in range(key_dev // LANES)], axis=1).astype(F32)
            count_wide = jnp.broadcast_to(count_row, (16, key_dev)).astype(BF16)
            st = s_ref[...].T
            st_ref[...] = st.reshape(st_ref.shape)
            scaled[...] = (st * count_wide[0:1]).reshape(scaled.shape)
        else:
            counts[...] += part
    pairs[:, :half] = split(counts[:key_dev], 0)
    pairs[:, half:] = split(counts[key_dev:], 0)

    pl.semaphore_wait(barrier, greeted)

    def remote(src, dst, send, recv, at, tile):
        return pltpu.make_async_remote_copy(
            src_ref=src, dst_ref=dst, send_sem=send, recv_sem=recv, device_id=(at, tile), device_id_type=MESH
        )

    def x_copy(src, dst, send, recv, k):
        return remote(src, dst, send, recv, g, (t + k) % X)

    def core_copy(src, dst, send, recv):
        return remote(src, dst, send, recv, key(z, y, 1 - c), t)

    def y_copy(src, dst, send, recv, k):
        return remote(src, dst, send, recv, key(z, (y + k) % Y, c), t)

    def z_copy(src, dst, send, recv, k, tile):
        return remote(src, dst, send, recv, key((z + k) % Z, y, c), tile)

    n_copies = []
    for k in range(1, X):
        n_copies.append(x_copy(n_part, n_recv.at[k - 1], n_send_sem.at[k - 1], n_recv_sem.at[k - 1], k))
        n_copies[-1].start()

    sides = (1, X - 1)
    chunk = cb // 2
    pair = key_dev // 2

    def half_rows(n):
        return pl.ds(n * pair, pair)

    def forward(q, side):
        return x_copy(
            a_part.at[2, q, half_rows(side)], f_recv.at[side, q],
            f_send_sem.at[side, q], f_recv_sem.at[side, q], sides[side],
        )

    def direct(q, side, n):
        return x_copy(
            a_part.at[sides[side], q, half_rows(n)], a_recv.at[side, q, half_rows(n)],
            a_send_sem.at[side, q, n], a_recv_sem.at[side, q, n], sides[side],
        )

    def aggregate_block(k):
        cols = pl.ds(pl.multiple_of(item_block((t + k) % X) * cb, cb), cb)
        both = dot(pairs[...], i_ref[:, cols])
        both = both[:key_dev] + both[key_dev:]
        for q in range(2):
            a_part[k, q] = both[:, q * chunk : (q + 1) * chunk]

    def pass_on(q):
        for side in range(2):
            forward(q, side).wait()
            a_part[sides[side], q, half_rows(side)] += f_recv[side, q]
            direct(q, side, side).start()

    loads[3].wait()
    aggregate_block(2)
    for side in range(2):
        forward(0, side).start()

    item_row = dot(jnp.concatenate([count_wide, count_wide], axis=1), pairs[...])
    for r in range(item_dev // LANES):
        w_part[0, r : r + 1, :] = item_row[0:1, r * LANES : (r + 1) * LANES]
    w_core = core_copy(w_part.at[0], w_recv.at[0], w_send_sem.at[0], w_recv_sem.at[0])
    w_core.start()

    for side in range(2):
        aggregate_block(sides[side])
        direct(0, side, 1 - side).start()
    for side in range(2):
        forward(1, side).start()
        direct(1, side, 1 - side).start()
    aggregate_block(0)

    w_core.wait()
    w_part[1] = w_part[0] + w_recv[0]
    w_copies = []
    for k in range(1, Y):
        w_copies.append(y_copy(w_part.at[1], w_recv.at[k], w_send_sem.at[k], w_recv_sem.at[k], k))
        w_copies[-1].start()

    def core_stage(bufs, left, right):
        part, recv, send_sem, recv_sem = bufs[:4]
        part[0] = dot(left(1 - c), right).reshape(part.shape[1:])
        copy = core_copy(part.at[0], recv, send_sem, recv_sem)
        copy.start()

    def own_stage(bufs, left, right):
        bufs[0][1] = dot(left(c), right).reshape(bufs[1].shape)

    def y_half(n):
        return pl.ds(n * (Z // 2), Z // 2)

    def y_forward(bufs, side):
        y_part, f_recv, _, f_send_sem, f_recv_sem = bufs[4:9]
        return y_copy(y_part.at[2, y_half(side)], f_recv.at[side], f_send_sem.at[side], f_recv_sem.at[side], sides[side])

    def y_direct(bufs, side, n):
        y_part, y_recv, y_send_sem, y_recv_sem = bufs[4], bufs[6], bufs[9], bufs[10]
        return y_copy(
            y_part.at[sides[side], y_half(n)], y_recv.at[side, y_half(n)],
            y_send_sem.at[side, n], y_recv_sem.at[side, n], sides[side],
        )

    def y_begin(bufs):
        part, recv, send_sem, recv_sem, y_part = bufs[:5]
        core_copy(part.at[0], recv, send_sem, recv_sem).wait()

        def add(k):
            at = (y + k) % Y
            y_part[k] = part[1, :, at] + recv[:, at]

        add(2)
        for side in range(2):
            y_forward(bufs, side).start()
        for side in range(2):
            add(sides[side])
            y_direct(bufs, side, 1 - side).start()
        add(0)

    def y_pass(bufs):
        y_part, f_recv = bufs[4:6]
        for side in range(2):
            y_forward(bufs, side).wait()
            y_part[sides[side], y_half(side)] += f_recv[side]
            y_direct(bufs, side, side).start()

    def y_end(bufs):
        y_part, y_recv, z_part = bufs[4], bufs[6], bufs[11]
        for side in range(2):
            for n in (1 - side, side):
                y_direct(bufs, side, n).wait()
        z_part[...] = y_part[0] + (y_recv[0] + y_recv[1])

    far_first = sorted(range(1, Z), key=lambda k: -min(k, Z - k))
    place = item_block(t) % 2
    store_place = store_block(t) % 2

    def unless_here(tile, src, dst, send, recv, copy):
        pl.when(tile != t)(copy.start)
        pl.when(tile == t)(pltpu.make_async_copy(src, dst, recv).start)
        return lambda: pl.when(tile != t)(copy.wait_send)

    def z_own(bufs, k):
        z_part, z_recv, z_send_sem, z_recv_sem = bufs[11:15]
        return z_copy(z_part.at[(z + k) % Z], z_recv.at[0, k], z_send_sem.at[k], z_recv_sem.at[0, k], k, t)

    def z_begin(bufs):
        y_end(bufs)
        for k in far_first:
            z_own(bufs, k).start()

    def z_end(bufs, kind):
        z_part, z_recv = bufs[11:13]
        part, recv, send_sem, recv_sem = bufs[15:]
        for k in far_first:
            z_own(bufs, k).wait()
        block = z_part[z]
        for k in range(1, Z):
            block += z_recv[0, k]
        part[...] = block
        tile = kind * (X // 2) + (item_block(t) if kind else store_block(t)) // 2
        copy = remote(part, recv.at[store_place], send_sem, recv_sem.at[store_place], g, tile)
        return unless_here(tile, part, recv.at[store_place], send_sem, recv_sem.at[store_place], copy)

    def landed(bufs, col, divisor):
        _, recv, send_sem, recv_sem = bufs[15:]
        width = recv.shape[-1]
        for at in range(2):
            remote(recv.at[at], recv.at[at], send_sem, recv_sem.at[at], g, t).wait_recv()
            left_ref[:, at * cb + col : at * cb + col + width] = recv[at] / divisor

    owner = X // 2 + item_block(t) // 2
    near_first = sorted(range(1, Y), key=lambda k: -min(k, Y - k))

    def item_y_copy(bufs, k):
        y_part, y_recv, send_sem, recv_sem = bufs[4:8]
        return y_copy(y_part.at[k], y_recv.at[k - 1], send_sem.at[k - 1], recv_sem.at[k - 1], k)

    def item_y(bufs):
        part, recv, send_sem, recv_sem, y_part = bufs[:5]
        core_copy(part.at[0], recv, send_sem, recv_sem).wait()
        for k in near_first + [0]:
            at = (y + k) % Y
            y_part[k] = part[1, :, at] + recv[:, at]
            if k:
                item_y_copy(bufs, k).start()

    def item_z(bufs):
        y_part, y_recv = bufs[4:6]
        z_part, z_recv, z_send_sem, z_recv_sem = bufs[8:]
        for k in near_first:
            item_y_copy(bufs, k).wait()
        block = y_part[0]
        for k in range(1, Y):
            block += y_recv[k - 1]
        z_part[...] = block
        sent = []
        for k in far_first + [0]:
            src, dst, send, got = z_part.at[(z + k) % Z], z_recv.at[place, k], z_send_sem.at[k], z_recv_sem.at[place, k]
            copy = z_copy(src, dst, send, got, k, owner)
            if k:
                copy.start()
                sent.append(copy.wait_send)
            else:
                sent.append(unless_here(owner, src, dst, send, got, copy))
        return sent

    def item_landed(bufs, col, divisor):
        _, recv, send_sem, recv_sem = bufs[8:]
        for at in range(2):
            for k in range(Z):
                slot = recv.at[at, k]
                remote(slot, slot, send_sem.at[k], recv_sem.at[at, k], g, t).wait_recv()
            block = recv[at, 0]
            for k in range(1, Z):
                block += recv[at, k]
            left_ref[:, at * cb + col : at * cb + col + chunk] = block / divisor

    for copy in n_copies:
        copy.wait()
    store_rows = n_part[...]
    for k in range(1, X):
        store_rows += n_recv[k - 1]
    weight_row = count_row * jnp.concatenate([store_rows[r : r + 1] for r in range(key_dev // LANES)], axis=1)

    def weighted(side):
        part = st_ref[:, :, side].reshape(-1, key_dev).astype(F32) * weight_row
        return split(part, 1)

    own = s_ref[:, pl.ds(pl.multiple_of(store_block(t) * cb, cb), cb)]
    own = jnp.concatenate([own, own], axis=0)
    core_stage(ss_bufs, weighted, own)

    pass_on(0)
    own_stage(ss_bufs, weighted, own)
    for copy in w_copies:
        copy.wait()
    total = w_part[1]
    for k in range(1, Y):
        total += w_recv[k]
    w_part[2] = total
    w_copies = []
    for k in range(1, Z):
        at = Y + k - 1
        w_copies.append(z_copy(w_part.at[2], w_recv.at[at], w_send_sem.at[at], w_recv_sem.at[at], k, t))
        w_copies[-1].start()

    y_begin(ss_bufs)

    pass_on(1)
    y_pass(ss_bufs)

    def counted(side):
        part = scaled[:, :, side].reshape(-1, key_dev)
        return jnp.concatenate([part, part], axis=1)

    def item_columns(q, bufs):
        for side in range(2):
            for n in range(2):
                direct(q, side, n).wait()
        right = split(a_part[0, q] + (a_recv[0, q] + a_recv[1, q]), 0)
        core_stage(bufs, counted, right)
        own_stage(bufs, counted, right)

    item_columns(0, sa0_bufs)

    item_y(sa0_bufs)
    item_columns(1, sa1_bufs)
    item_y(sa1_bufs)
    z_begin(ss_bufs)
    sents = item_z(sa0_bufs)

    for copy in w_copies:
        copy.wait()
    total = w_part[2]
    for k in range(1, Z):
        total += w_recv[Y + k - 1]
    weights = jnp.concatenate([total[r : r + 1, :] for r in range(item_dev // LANES)], axis=1)
    wide = max(rows, LANES)
    block = i_ref[:, pl.ds(pl.multiple_of(((g * rows) // wide) * wide, wide), wide)]
    first = (g * rows) % wide
    pick = lax.broadcasted_iota(jnp.int32, (rows, wide), 1) == lax.broadcasted_iota(jnp.int32, (rows, wide), 0) + first
    picked = nt_dot(jnp.where(pick, 1.0, 0.0).astype(BF16), block)
    both = dot(split(picked * weights, 0), i_ref[...])
    item_rows = both[:rows] + both[rows:]
    for at in range(X):
        g_part[at, :rows] = item_rows[:, at * cb : (at + 1) * cb]
        g_part[at, rows:] = jnp.broadcast_to(jnp.sum(total), (8, cb))
    g_copies = []
    for k in range(1, X):
        g_copies.append(
            x_copy(g_part.at[(t + k) % X], g_recv.at[k - 1], g_send_sem.at[k - 1], g_recv_sem.at[k - 1], k)
        )
        g_copies[-1].start()

    sents.append(z_end(ss_bufs, 0))
    sents += item_z(sa1_bufs)

    for copy in g_copies:
        copy.wait()
    item_rows = g_part[t]
    for k in range(1, X):
        item_rows += g_recv[k - 1]
    total = item_rows[rows : rows + 1, :chunk]
    gram_ref[...] = item_rows[:rows] / item_rows[rows : rows + 1]

    @pl.when(t < X // 2)
    def _():
        landed(ss_bufs, 0, item_rows[rows : rows + 1])

    @pl.when(t >= X // 2)
    def _():
        item_landed(sa0_bufs, 0, total)
        item_landed(sa1_bufs, chunk, total)

    for sent in sents:
        sent()


def shards(y_size, fact_store, fact_item, store_count, store_table, item_table):
    key_dev, width_a = store_table.shape
    item_dev, width_b = item_table.shape
    X = lax.axis_size("tiles")
    keys_count = lax.axis_size("keys")
    Y = y_size
    Z = keys_count // (CORES * Y)
    rows, cb = width_a // keys_count, width_b // X
    facts = fact_store.shape[0]
    vmem, dma = pltpu.VMEM, pltpu.SemaphoreType.DMA

    def reduction(width):
        return (
            vmem((2, Z, Y, rows, width), F32), vmem((Z, Y, rows, width), F32), dma(()), dma(()),
            vmem((Y, Z, rows, width), F32), vmem((2, Z // 2, rows, width), F32), vmem((2, Z, rows, width), F32),
            dma((2,)), dma((2,)), dma((2, 2)), dma((2, 2)),
            vmem((Z, rows, width), F32), vmem((1, Z, rows, width), F32), dma((Z,)), dma((1, Z)),
            vmem((rows, width), F32), vmem((2, rows, width), F32), dma(()), dma((2,)),
        )

    def item_reduction(width):
        return (
            vmem((2, Z, Y, rows, width), F32), vmem((Z, Y, rows, width), F32), dma(()), dma(()),
            vmem((Y, Z, rows, width), F32), vmem((Y - 1, Z, rows, width), F32), dma((Y - 1,)), dma((Y - 1,)),
            vmem((Z, rows, width), F32), vmem((2, Z, rows, width), F32), dma((Z,)), dma((2, Z)),
        )

    scratch = [
        vmem((facts // LANES, LANES), jnp.int32), vmem((facts // LANES, LANES), jnp.int32),
        vmem((key_dev // LANES, LANES), jnp.int32),
        vmem((key_dev, width_a), BF16), vmem((item_dev, width_b), BF16), dma((5,)),
        vmem((2 * key_dev, item_dev // 2), F32), vmem((2 * key_dev, item_dev), BF16),
        vmem((Z, Y, CORES, rows, key_dev), BF16), vmem((Z, Y, CORES, rows, key_dev), BF16),
        vmem((16, LANES), F32), vmem((X - 1, 16, LANES), F32), dma((X - 1,)), dma((X - 1,)),
        vmem((X, 2, key_dev, cb // 2), F32), vmem((2, 2, key_dev // 2, cb // 2), F32),
        vmem((2, 2, key_dev, cb // 2), F32), dma((2, 2)), dma((2, 2)), dma((2, 2, 2)), dma((2, 2, 2)),
        reduction(cb), item_reduction(cb // 2), item_reduction(cb // 2),
        vmem((3, 8, item_dev // 8), F32), vmem((Y + Z - 1, 8, item_dev // 8), F32),
        dma((Y + Z - 1,)), dma((Y + Z - 1,)),
        vmem((X, rows + 8, cb), F32), vmem((X - 1, rows + 8, cb), F32), dma((X - 1,)), dma((X - 1,)),
    ]
    whole = pl.BlockSpec(memory_space=pltpu.VMEM)
    hbm = pl.BlockSpec(memory_space=pltpu.HBM)
    return pl.pallas_call(
        functools.partial(kernel, (X, Y, Z, key_dev, item_dev, cb, rows)),
        out_shape=[
            jax.ShapeDtypeStruct((rows, 2 * cb), F32),
            jax.ShapeDtypeStruct((rows, cb), F32),
        ],
        in_specs=[hbm] * 5,
        out_specs=[whole, whole],
        scratch_shapes=scratch,
        compiler_params=pltpu.CompilerParams(
            collective_id=0, has_side_effects=True, vmem_limit_bytes=40 * 1024 * 1024
        ),
    )(
        *(
            pltpu.with_memory_space_constraint(operand, pltpu.HBM)
            for operand in (
                fact_store.reshape(facts // LANES, LANES),
                fact_item.reshape(facts // LANES, LANES),
                store_count.reshape(key_dev // LANES, LANES),
                store_table,
                item_table,
            )
        )
    )


def solution(mesh, y_size=4):
    placed = (
        P(("keys", "tiles")),
        P(("keys", "tiles")),
        P("keys"),
        P("keys", None),
        P("tiles", None),
    )
    return jax.shard_map(
        functools.partial(shards, y_size),
        mesh=mesh,
        in_specs=placed,
        out_specs=(P("keys", "tiles"), P("keys", "tiles")),
        check_vma=False,
    )
```

```python
import functools

import jax
import jax.numpy as jnp
from jax import lax
from jax.experimental import pallas as pl
from jax.experimental.pallas import tpu as pltpu
from jax.sharding import PartitionSpec as P

MESH = pl.DeviceIdType.MESH
F32 = jnp.float32
BF16 = jnp.bfloat16
F8 = jnp.float8_e4m3fn
CORES = 2
LANES = 128


def nt_dot(a, b):
    return lax.dot_general(a, b, (((1,), (1,)), ((), ())), preferred_element_type=F32)


def dot(a, b):
    return jnp.dot(a, b, preferred_element_type=F32)


def split(x, axis):
    high = x.astype(BF16)
    low = (x - high.astype(F32)).astype(BF16)
    return jnp.concatenate([high, low], axis=axis)


def kernel(
    dims,
    fs_hbm, fi_hbm, sc_hbm, s_hbm, i_hbm,
    left_ref, gram_ref,
    fs_ref, fi_ref, sc_ref, s_ref, i_ref, in_sem,
    counts, pairs, st_ref, scaled,
    n_part, n_recv, n_send_sem, n_recv_sem,
    a_part, f_recv, a_recv, f_send_sem, f_recv_sem, a_send_sem, a_recv_sem,
    ss_bufs, sa0_bufs, sa1_bufs,
    w_part, w_recv, w_send_sem, w_recv_sem,
    g_part, g_recv, g_send_sem, g_recv_sem,
):
    X, Y, Z, key_dev, item_dev, cb, rows = dims
    g = lax.axis_index("keys")
    t = lax.axis_index("tiles")
    c = g % CORES
    y = (g // CORES) % Y
    z = g // (CORES * Y)

    def store_block(tile):
        upper = tile // 2
        return (1 - upper) * 2 * tile + upper * (7 - 2 * tile)

    def item_block(tile):
        upper = tile // 2
        return (1 - upper) * (3 - 2 * tile) + upper * (2 * tile - 4)

    def key(z_at, y_at, c_at):
        return (z_at * Y + y_at) * CORES + c_at

    loads = [
        pltpu.make_async_copy(src, dst, in_sem.at[n])
        for n, (src, dst) in enumerate(
            ((fs_hbm, fs_ref), (fi_hbm, fi_ref), (sc_hbm, sc_ref), (i_hbm, i_ref), (s_hbm, s_ref))
        )
    ]
    for load in loads:
        load.start()

    barrier = pltpu.get_barrier_semaphore()
    greeted = 0
    partners = [(key(z, y, c), (t + dx) % X) for dx in range(1, X)] + [(key(z, y, 1 - c), t)]
    partners += [(key(z, (y + dy) % Y, c), t) for dy in range(1, Y)]
    partners += [(key((z + dz) % Z, y, c), (t + dx) % X) for dx in range(X) for dz in range(1, Z)]
    for at, tile in partners:
        pl.semaphore_signal(barrier, inc=1, device_id=(at, tile), device_id_type=MESH)
        greeted += 1

    loads[0].wait()
    loads[1].wait()
    half = item_dev // 2
    local_store = fs_ref[...] - g * key_dev
    local_item = fi_ref[...] - t * item_dev
    upper = jnp.where(local_item >= half, 1, 0)
    u = (upper * key_dev + local_store - 256).astype(F32)
    v = (local_item - upper * half - 256).astype(F32)
    iota = (lax.broadcasted_iota(jnp.int32, (512, LANES), 0) - 256).astype(F32).astype(BF16)
    iota = iota.reshape(32, 16, LANES)

    def hot(row):
        row = jnp.broadcast_to(row, (16, LANES)).astype(BF16)
        one = jnp.where(iota == row[None], jnp.ones((), BF16), jnp.zeros((), BF16))
        return one.reshape(512, LANES).astype(F8)

    store_low = (local_store % LANES).astype(F32)
    store_high = (local_store // LANES).astype(F32)
    count = lax.broadcasted_iota(jnp.int32, (LANES, LANES), 0).astype(F32).astype(BF16).reshape(-1, 16, LANES)

    def hot_store(row, groups):
        row = jnp.broadcast_to(row, (16, LANES)).astype(BF16)
        one = jnp.where(count[:groups] == row[None], jnp.ones((), BF16), jnp.zeros((), BF16))
        return one.reshape(16 * groups, LANES)

    steps = fs_ref.shape[0]
    n_part[...] = nt_dot(
        jnp.concatenate([hot_store(store_high[r : r + 1], 1) for r in range(steps)], axis=1),
        jnp.concatenate([hot_store(store_low[r : r + 1], LANES // 16) for r in range(steps)], axis=1),
    )

    per = 8
    for step in range(steps // per):
        at = range(step * per, step * per + per)
        hot_u = jnp.concatenate([hot(u[r : r + 1]) for r in at], axis=1)
        hot_v = jnp.concatenate([hot(v[r : r + 1]) for r in at], axis=1)
        part = nt_dot(hot_u, hot_v)
        if step == 0:
            counts[...] = part
            loads[2].wait()
            loads[4].wait()
            count_row = jnp.concatenate([sc_ref[r : r + 1, :] for r in range(key_dev // LANES)], axis=1).astype(F32)
            count_wide = jnp.broadcast_to(count_row, (16, key_dev)).astype(BF16)
            st = s_ref[...].T
            st_ref[...] = st.reshape(st_ref.shape)
            scaled[...] = (st * count_wide[0:1]).reshape(scaled.shape)
        else:
            counts[...] += part
    pairs[:, :half] = split(counts[:key_dev], 0)
    pairs[:, half:] = split(counts[key_dev:], 0)

    pl.semaphore_wait(barrier, greeted)

    def remote(src, dst, send, recv, at, tile):
        return pltpu.make_async_remote_copy(
            src_ref=src, dst_ref=dst, send_sem=send, recv_sem=recv, device_id=(at, tile), device_id_type=MESH
        )

    def x_copy(src, dst, send, recv, k):
        return remote(src, dst, send, recv, g, (t + k) % X)

    def core_copy(src, dst, send, recv):
        return remote(src, dst, send, recv, key(z, y, 1 - c), t)

    def y_copy(src, dst, send, recv, k):
        return remote(src, dst, send, recv, key(z, (y + k) % Y, c), t)

    def z_copy(src, dst, send, recv, k, tile):
        return remote(src, dst, send, recv, key((z + k) % Z, y, c), tile)

    n_copies = []
    for k in range(1, X):
        n_copies.append(x_copy(n_part, n_recv.at[k - 1], n_send_sem.at[k - 1], n_recv_sem.at[k - 1], k))
        n_copies[-1].start()

    sides = (1, X - 1)
    chunk = cb // 2
    pair = key_dev // 2

    def half_rows(n):
        return pl.ds(n * pair, pair)

    def forward(q, side):
        return x_copy(
            a_part.at[2, q, half_rows(side)], f_recv.at[side, q],
            f_send_sem.at[side, q], f_recv_sem.at[side, q], sides[side],
        )

    def direct(q, side, n):
        return x_copy(
            a_part.at[sides[side], q, half_rows(n)], a_recv.at[side, q, half_rows(n)],
            a_send_sem.at[side, q, n], a_recv_sem.at[side, q, n], sides[side],
        )

    def aggregate_block(k):
        cols = pl.ds(pl.multiple_of(item_block((t + k) % X) * cb, cb), cb)
        both = dot(pairs[...], i_ref[:, cols])
        both = both[:key_dev] + both[key_dev:]
        for q in range(2):
            a_part[k, q] = both[:, q * chunk : (q + 1) * chunk]

    def pass_on(q):
        for side in range(2):
            forward(q, side).wait()
            a_part[sides[side], q, half_rows(side)] += f_recv[side, q]
            direct(q, side, side).start()

    loads[3].wait()
    aggregate_block(2)
    for side in range(2):
        forward(0, side).start()

    item_row = dot(jnp.concatenate([count_wide, count_wide], axis=1), pairs[...])
    for r in range(item_dev // LANES):
        w_part[0, r : r + 1, :] = item_row[0:1, r * LANES : (r + 1) * LANES]
    w_core = core_copy(w_part.at[0], w_recv.at[0], w_send_sem.at[0], w_recv_sem.at[0])
    w_core.start()

    for side in range(2):
        aggregate_block(sides[side])
        direct(0, side, 1 - side).start()
    for side in range(2):
        forward(1, side).start()
        direct(1, side, 1 - side).start()
    aggregate_block(0)

    w_core.wait()
    w_part[1] = w_part[0] + w_recv[0]
    w_copies = []
    for k in range(1, Y):
        w_copies.append(y_copy(w_part.at[1], w_recv.at[k], w_send_sem.at[k], w_recv_sem.at[k], k))
        w_copies[-1].start()

    def core_stage(bufs, left, right):
        part, recv, send_sem, recv_sem = bufs[:4]
        part[0] = dot(left(1 - c), right).reshape(part.shape[1:])
        copy = core_copy(part.at[0], recv, send_sem, recv_sem)
        copy.start()

    def own_stage(bufs, left, right):
        bufs[0][1] = dot(left(c), right).reshape(bufs[1].shape)

    def y_half(n):
        return pl.ds(n * (Z // 2), Z // 2)

    def y_forward(bufs, side):
        y_part, f_recv, _, f_send_sem, f_recv_sem = bufs[4:9]
        return y_copy(y_part.at[2, y_half(side)], f_recv.at[side], f_send_sem.at[side], f_recv_sem.at[side], sides[side])

    def y_direct(bufs, side, n):
        y_part, y_recv, y_send_sem, y_recv_sem = bufs[4], bufs[6], bufs[9], bufs[10]
        return y_copy(
            y_part.at[sides[side], y_half(n)], y_recv.at[side, y_half(n)],
            y_send_sem.at[side, n], y_recv_sem.at[side, n], sides[side],
        )

    def y_begin(bufs):
        part, recv, send_sem, recv_sem, y_part = bufs[:5]
        core_copy(part.at[0], recv, send_sem, recv_sem).wait()

        def add(k):
            at = (y + k) % Y
            y_part[k] = part[1, :, at] + recv[:, at]

        add(2)
        for side in range(2):
            y_forward(bufs, side).start()
        for side in range(2):
            add(sides[side])
            y_direct(bufs, side, 1 - side).start()
        add(0)

    def y_pass(bufs):
        y_part, f_recv = bufs[4:6]
        for side in range(2):
            y_forward(bufs, side).wait()
            y_part[sides[side], y_half(side)] += f_recv[side]
            y_direct(bufs, side, side).start()

    def y_end(bufs):
        y_part, y_recv, z_part = bufs[4], bufs[6], bufs[11]
        for side in range(2):
            for n in (1 - side, side):
                y_direct(bufs, side, n).wait()
        z_part[...] = y_part[0] + (y_recv[0] + y_recv[1])

    far_first = sorted(range(1, Z), key=lambda k: -min(k, Z - k))
    place = item_block(t) % 2
    store_place = store_block(t) % 2

    def unless_here(tile, src, dst, send, recv, copy):
        pl.when(tile != t)(copy.start)
        pl.when(tile == t)(pltpu.make_async_copy(src, dst, recv).start)
        return lambda: pl.when(tile != t)(copy.wait_send)

    def z_own(bufs, k):
        z_part, z_recv, z_send_sem, z_recv_sem = bufs[11:15]
        return z_copy(z_part.at[(z + k) % Z], z_recv.at[0, k], z_send_sem.at[k], z_recv_sem.at[0, k], k, t)

    def z_begin(bufs):
        y_end(bufs)
        for k in far_first:
            z_own(bufs, k).start()

    def z_end(bufs, kind):
        z_part, z_recv = bufs[11:13]
        part, recv, send_sem, recv_sem = bufs[15:]
        for k in far_first:
            z_own(bufs, k).wait()
        block = z_part[z]
        for k in range(1, Z):
            block += z_recv[0, k]
        part[...] = block
        tile = kind * (X // 2) + (item_block(t) if kind else store_block(t)) // 2
        copy = remote(part, recv.at[store_place], send_sem, recv_sem.at[store_place], g, tile)
        return unless_here(tile, part, recv.at[store_place], send_sem, recv_sem.at[store_place], copy)

    def landed(bufs, col, divisor):
        _, recv, send_sem, recv_sem = bufs[15:]
        width = recv.shape[-1]
        for at in range(2):
            remote(recv.at[at], recv.at[at], send_sem, recv_sem.at[at], g, t).wait_recv()
            left_ref[:, at * cb + col : at * cb + col + width] = recv[at] / divisor

    owner = X // 2 + item_block(t) // 2
    near_first = sorted(range(1, Y), key=lambda k: -min(k, Y - k))

    def item_y_copy(bufs, k):
        y_part, y_recv, send_sem, recv_sem = bufs[4:8]
        return y_copy(y_part.at[k], y_recv.at[k - 1], send_sem.at[k - 1], recv_sem.at[k - 1], k)

    def item_y(bufs):
        part, recv, send_sem, recv_sem, y_part = bufs[:5]
        core_copy(part.at[0], recv, send_sem, recv_sem).wait()
        for k in near_first + [0]:
            at = (y + k) % Y
            y_part[k] = part[1, :, at] + recv[:, at]
            if k:
                item_y_copy(bufs, k).start()

    def item_z(bufs):
        y_part, y_recv = bufs[4:6]
        z_part, z_recv, z_send_sem, z_recv_sem = bufs[8:]
        for k in near_first:
            item_y_copy(bufs, k).wait()
        block = y_part[0]
        for k in range(1, Y):
            block += y_recv[k - 1]
        z_part[...] = block
        sent = []
        for k in far_first + [0]:
            src, dst, send, got = z_part.at[(z + k) % Z], z_recv.at[place, k], z_send_sem.at[k], z_recv_sem.at[place, k]
            copy = z_copy(src, dst, send, got, k, owner)
            if k:
                copy.start()
                sent.append(copy.wait_send)
            else:
                sent.append(unless_here(owner, src, dst, send, got, copy))
        return sent

    def item_landed(bufs, col, divisor):
        _, recv, send_sem, recv_sem = bufs[8:]
        for at in range(2):
            for k in range(Z):
                slot = recv.at[at, k]
                remote(slot, slot, send_sem.at[k], recv_sem.at[at, k], g, t).wait_recv()
            block = recv[at, 0]
            for k in range(1, Z):
                block += recv[at, k]
            left_ref[:, at * cb + col : at * cb + col + chunk] = block / divisor

    for copy in n_copies:
        copy.wait()
    store_rows = n_part[...]
    for k in range(1, X):
        store_rows += n_recv[k - 1]
    weight_row = count_row * jnp.concatenate([store_rows[r : r + 1] for r in range(key_dev // LANES)], axis=1)

    def weighted(side):
        part = st_ref[:, :, side].reshape(-1, key_dev).astype(F32) * weight_row
        return split(part, 1)

    own = s_ref[:, pl.ds(pl.multiple_of(store_block(t) * cb, cb), cb)]
    own = jnp.concatenate([own, own], axis=0)
    core_stage(ss_bufs, weighted, own)

    pass_on(0)
    own_stage(ss_bufs, weighted, own)
    for copy in w_copies:
        copy.wait()
    total = w_part[1]
    for k in range(1, Y):
        total += w_recv[k]
    w_part[2] = total
    w_copies = []
    for k in range(1, Z):
        at = Y + k - 1
        w_copies.append(z_copy(w_part.at[2], w_recv.at[at], w_send_sem.at[at], w_recv_sem.at[at], k, t))
        w_copies[-1].start()

    y_begin(ss_bufs)

    pass_on(1)
    y_pass(ss_bufs)

    def counted(side):
        part = scaled[:, :, side].reshape(-1, key_dev)
        return jnp.concatenate([part, part], axis=1)

    def item_columns(q, bufs):
        for side in range(2):
            for n in range(2):
                direct(q, side, n).wait()
        right = split(a_part[0, q] + (a_recv[0, q] + a_recv[1, q]), 0)
        core_stage(bufs, counted, right)
        own_stage(bufs, counted, right)

    item_columns(0, sa0_bufs)

    item_y(sa0_bufs)
    item_columns(1, sa1_bufs)
    item_y(sa1_bufs)
    for copy in w_copies:
        copy.wait()
    total = w_part[2]
    for k in range(1, Z):
        total += w_recv[Y + k - 1]
    weights = jnp.concatenate([total[r : r + 1, :] for r in range(item_dev // LANES)], axis=1)
    wide = max(rows, LANES)
    block = i_ref[:, pl.ds(pl.multiple_of(((g * rows) // wide) * wide, wide), wide)]
    first = (g * rows) % wide
    pick = lax.broadcasted_iota(jnp.int32, (rows, wide), 1) == lax.broadcasted_iota(jnp.int32, (rows, wide), 0) + first
    picked = nt_dot(jnp.where(pick, 1.0, 0.0).astype(BF16), block)
    both = dot(split(picked * weights, 0), i_ref[...])
    item_rows = both[:rows] + both[rows:]
    for at in range(X):
        g_part[at, :rows] = item_rows[:, at * cb : (at + 1) * cb]
        g_part[at, rows:] = jnp.broadcast_to(jnp.sum(total), (8, cb))
    g_copies = []
    for k in range(1, X):
        g_copies.append(
            x_copy(g_part.at[(t + k) % X], g_recv.at[k - 1], g_send_sem.at[k - 1], g_recv_sem.at[k - 1], k)
        )
        g_copies[-1].start()
    z_begin(ss_bufs)
    sents = item_z(sa0_bufs)

    sents.append(z_end(ss_bufs, 0))
    sents += item_z(sa1_bufs)

    for copy in g_copies:
        copy.wait()
    item_rows = g_part[t]
    for k in range(1, X):
        item_rows += g_recv[k - 1]
    total = item_rows[rows : rows + 1, :chunk]
    gram_ref[...] = item_rows[:rows] / item_rows[rows : rows + 1]

    @pl.when(t < X // 2)
    def _():
        landed(ss_bufs, 0, item_rows[rows : rows + 1])

    @pl.when(t >= X // 2)
    def _():
        item_landed(sa0_bufs, 0, total)
        item_landed(sa1_bufs, chunk, total)

    for sent in sents:
        sent()


def shards(y_size, fact_store, fact_item, store_count, store_table, item_table):
    key_dev, width_a = store_table.shape
    item_dev, width_b = item_table.shape
    X = lax.axis_size("tiles")
    keys_count = lax.axis_size("keys")
    Y = y_size
    Z = keys_count // (CORES * Y)
    rows, cb = width_a // keys_count, width_b // X
    facts = fact_store.shape[0]
    vmem, dma = pltpu.VMEM, pltpu.SemaphoreType.DMA

    def reduction(width):
        return (
            vmem((2, Z, Y, rows, width), F32), vmem((Z, Y, rows, width), F32), dma(()), dma(()),
            vmem((Y, Z, rows, width), F32), vmem((2, Z // 2, rows, width), F32), vmem((2, Z, rows, width), F32),
            dma((2,)), dma((2,)), dma((2, 2)), dma((2, 2)),
            vmem((Z, rows, width), F32), vmem((1, Z, rows, width), F32), dma((Z,)), dma((1, Z)),
            vmem((rows, width), F32), vmem((2, rows, width), F32), dma(()), dma((2,)),
        )

    def item_reduction(width):
        return (
            vmem((2, Z, Y, rows, width), F32), vmem((Z, Y, rows, width), F32), dma(()), dma(()),
            vmem((Y, Z, rows, width), F32), vmem((Y - 1, Z, rows, width), F32), dma((Y - 1,)), dma((Y - 1,)),
            vmem((Z, rows, width), F32), vmem((2, Z, rows, width), F32), dma((Z,)), dma((2, Z)),
        )

    scratch = [
        vmem((facts // LANES, LANES), jnp.int32), vmem((facts // LANES, LANES), jnp.int32),
        vmem((key_dev // LANES, LANES), jnp.int32),
        vmem((key_dev, width_a), BF16), vmem((item_dev, width_b), BF16), dma((5,)),
        vmem((2 * key_dev, item_dev // 2), F32), vmem((2 * key_dev, item_dev), BF16),
        vmem((Z, Y, CORES, rows, key_dev), BF16), vmem((Z, Y, CORES, rows, key_dev), BF16),
        vmem((16, LANES), F32), vmem((X - 1, 16, LANES), F32), dma((X - 1,)), dma((X - 1,)),
        vmem((X, 2, key_dev, cb // 2), F32), vmem((2, 2, key_dev // 2, cb // 2), F32),
        vmem((2, 2, key_dev, cb // 2), F32), dma((2, 2)), dma((2, 2)), dma((2, 2, 2)), dma((2, 2, 2)),
        reduction(cb), item_reduction(cb // 2), item_reduction(cb // 2),
        vmem((3, 8, item_dev // 8), F32), vmem((Y + Z - 1, 8, item_dev // 8), F32),
        dma((Y + Z - 1,)), dma((Y + Z - 1,)),
        vmem((X, rows + 8, cb), F32), vmem((X - 1, rows + 8, cb), F32), dma((X - 1,)), dma((X - 1,)),
    ]
    whole = pl.BlockSpec(memory_space=pltpu.VMEM)
    hbm = pl.BlockSpec(memory_space=pltpu.HBM)
    return pl.pallas_call(
        functools.partial(kernel, (X, Y, Z, key_dev, item_dev, cb, rows)),
        out_shape=[
            jax.ShapeDtypeStruct((rows, 2 * cb), F32),
            jax.ShapeDtypeStruct((rows, cb), F32),
        ],
        in_specs=[hbm] * 5,
        out_specs=[whole, whole],
        scratch_shapes=scratch,
        compiler_params=pltpu.CompilerParams(
            collective_id=0, has_side_effects=True, vmem_limit_bytes=40 * 1024 * 1024
        ),
    )(
        *(
            pltpu.with_memory_space_constraint(operand, pltpu.HBM)
            for operand in (
                fact_store.reshape(facts // LANES, LANES),
                fact_item.reshape(facts // LANES, LANES),
                store_count.reshape(key_dev // LANES, LANES),
                store_table,
                item_table,
            )
        )
    )


def solution(mesh, y_size=4):
    placed = (
        P(("keys", "tiles")),
        P(("keys", "tiles")),
        P("keys"),
        P("keys", None),
        P("tiles", None),
    )
    return jax.shard_map(
        functools.partial(shards, y_size),
        mesh=mesh,
        in_specs=placed,
        out_specs=(P("keys", "tiles"), P("keys", "tiles")),
        check_vma=False,
    )
```
